256 devices in a mesh: ctx: 4 (over z_hi), tp: 8 (over y, core), dec: 8 (over x, z_lo).
Axes of the slice: x: 4, y: 4, z: 8 (z_hi: 4, z_lo: 2; z = z_hi * 2 + z_lo), core: 2. Of those that a mesh axis runs over, the one named last changes fastest.
Arguments:
- cache: bfloat16 [8, 1024, 576], P('dec', 'ctx'), may hold values from -6 to 6
- lengths: int32 [8], P('dec'), may hold values from 1 to 1024
- slot_sequence: int32 [8], replicated, may hold values from 0 to 7, each once
- parents: int32 [8, 64], P('dec'), may hold values from 0 to 62, as said below
- query_nope: bfloat16 [8, 64, 128, 128], P('dec', None, 'tp'), may hold values from -6 to 6
- query_rope: bfloat16 [8, 64, 128, 64], P('dec', None, 'tp'), may hold values from -90 to 90
- new_latent: bfloat16 [8, 64, 576], P('dec'), may hold values from -6 to 6
- key_up: bfloat16 [128, 128, 512], P('tp'), may hold values from -0.5 to 0.5
- value_up: bfloat16 [128, 512, 128], P('tp'), may hold values from -0.25 to 0.25
- out_proj: bfloat16 [16384, 7168], P('tp', ('ctx', 'dec')), may hold values from -0.046875 to 0.046875
Outputs:
- attended: bfloat16 [8, 64, 7168], P(None, 'tp', ('ctx', 'dec'))
The draws below stay inside these ranges and needn't reach their ends.
Inputs may be any that keep to these rules, and one draw needn't show every extreme that they name: `slot_sequence`: every sequence is held by exactly one slot. parents[s, 0] = 0 and parents[s, i] < i for every i >= 1.
All inputs are finite; a program needn't handle non-finite values.
Results may differ from the reference program's by a relative error of at most 0.024.
Values may be sent and summed in bfloat16 or wider, within the bound.
A program may use at most 64 MiB of HBM per device.

```python
import math
import jax
import jax.numpy as jnp
from jax import lax

D = 7168
H = 128
HD = 128
RD = 64
LAT = 512
VD = 128
NODES = 64
SEQS = 8
CACHE = 1024


def shared_tree(key):
    latent_key, rope_key = jax.random.split(key, 2)
    latent_rows = jnp.clip(jax.random.normal(latent_key, (SEQS, NODES, LAT + RD), jnp.float32), -6.0, 6.0)
    rope_rows = jnp.clip(jax.random.normal(rope_key, (SEQS, NODES, H, RD), jnp.float32), -6.0, 6.0)
    return (latent_rows, rope_rows)


def draw_new_latent(key, part):
    return shared_tree(jax.random.fold_in(key, 7))[0].astype(jnp.bfloat16)


def draw_query_rope(key, part):
    return shared_tree(jax.random.fold_in(key, 7))[1].astype(jnp.bfloat16)


def draw_parents(key, part):
    node_ids = jnp.arange(NODES, dtype=jnp.int32)
    upper = jnp.broadcast_to(jnp.maximum(node_ids, 1)[None, :], (SEQS, NODES))
    return jax.random.randint(key, (SEQS, NODES), 0, upper).astype(jnp.int32)


def set_ends(array, own_key, low, largest):
    spot = [jax.random.randint(jax.random.fold_in(own_key, axis), (), 0, length) for axis, length in enumerate(array.shape)]
    widest = array.shape.index(max(array.shape))
    beside = spot[:widest] + [(spot[widest] + 1) % array.shape[widest]] + spot[widest + 1:]
    return array.at[tuple(spot)].set(low).at[tuple(beside)].set(largest)


def block_levels(rng, dims, pieces, smallest, high):
    level = 1.0
    for position, parts in pieces:
        steps = jax.random.uniform(jax.random.fold_in(jax.random.fold_in(rng, 6), position), (parts,), jnp.float32, smallest / len(pieces), high / len(pieces))
        level = level * jnp.repeat(jnp.exp(steps), dims[position] // parts).reshape((-1,) + (1,) * (len(dims) - 1 - position))
    return level


def gaussian(key, shape, deviation, bound, cuts=(), held_as=jnp.bfloat16):
    values = jax.random.normal(key, shape, jnp.float32) * deviation
    if len(cuts) > 0:
        values = block_levels(key, shape, cuts, -0.22, 0.18) * values
    return jnp.clip(values, min=-bound, max=bound).astype(held_as)


def setup_inputs(seed: int = 0) -> dict:
    key_of = jax.random.split(jax.random.key(seed), 11)
    cache = gaussian(key_of[0], (SEQS, CACHE, LAT + RD), 1.0, 6.0, ((0, 8), (1, 4)))
    lengths = set_ends(jax.random.randint(key_of[1], (SEQS,), 1, CACHE + 1), jax.random.fold_in(key_of[1], 1), 1, CACHE).astype(jnp.int32)
    slot_sequence = jax.random.permutation(key_of[2], SEQS).astype(jnp.int32)
    parents = draw_parents(jax.random.fold_in(key_of[10], 71), 0)
    query_nope = gaussian(key_of[4], (SEQS, NODES, H, HD), 1.0, 6.0, ((0, 8), (2, 8)))
    query_rope = draw_query_rope(jax.random.fold_in(key_of[10], 71), 0)
    new_latent = draw_new_latent(jax.random.fold_in(key_of[10], 71), 0)
    key_up = gaussian(key_of[7], (H, HD, LAT), HD ** -0.5, 0.5, ((0, 8),))
    value_up = gaussian(key_of[8], (H, LAT, VD), LAT ** -0.5, 0.25, ((0, 8),))
    out_proj = gaussian(key_of[9], (H * VD, D), (H * VD) ** -0.5, 0.046875, ((0, 8), (1, 32)))
    return {"cache": cache, "lengths": lengths, "slot_sequence": slot_sequence, "parents": parents, "query_nope": query_nope, "query_rope": query_rope, "new_latent": new_latent, "key_up": key_up, "value_up": value_up, "out_proj": out_proj}


def ancestors(parents):
    node_count = parents.shape[-1]
    node_ids = jnp.arange(node_count, dtype=jnp.int32)
    parent_link = (parents[..., :, None] == node_ids).astype(jnp.float32)
    closure = jnp.maximum(parent_link, jnp.eye(node_count, dtype=jnp.float32))
    for _ in range(node_count.bit_length()):
        closure = jnp.minimum(jnp.einsum('sij,sjk->sik', closure, closure, precision=lax.Precision.HIGHEST), 1.0)
    return closure

def reference(cache, lengths, slot_sequence, parents, query_nope, query_rope, new_latent, key_up, value_up, out_proj):
    score_scale = 1.0 / math.sqrt(HD + RD)
    tree_mask = ancestors(parents)
    positions = jnp.arange(CACHE, dtype=jnp.int32)
    key_weight = key_up.astype(jnp.float32)
    value_weight = value_up.astype(jnp.float32)

    def per_slot(slot_index):
        sequence = slot_sequence[slot_index]
        cache_rows = lax.dynamic_index_in_dim(cache, sequence, 0, keepdims=False).astype(jnp.float32)
        length = lax.dynamic_index_in_dim(lengths, sequence, 0, keepdims=False)
        absorbed = jnp.einsum('nhd,hdc->nhc', query_nope[slot_index].astype(jnp.float32), key_weight).astype(jnp.bfloat16)
        queries = lax.optimization_barrier(jnp.concatenate([absorbed, query_rope[slot_index]], axis=-1)).astype(jnp.float32)
        tree_rows = new_latent[slot_index].astype(jnp.float32)
        cache_scores = jnp.einsum('nhc,pc->nhp', queries, cache_rows) * score_scale
        tree_scores = jnp.einsum('nhc,pc->nhp', queries, tree_rows) * score_scale
        cache_live = (positions < length)[None, None, :]
        tree_live = (tree_mask[slot_index] > 0)[:, None, :]
        cache_scores = jnp.where(cache_live, cache_scores, -1e+30)
        tree_scores = jnp.where(tree_live, tree_scores, -1e+30)
        row_peak = jnp.maximum(lax.optimization_barrier(jnp.max(cache_scores, axis=-1)), lax.optimization_barrier(jnp.max(tree_scores, axis=-1)))
        cache_expo = jnp.where(cache_live, jnp.exp(cache_scores - row_peak[..., None]), 0.0)
        tree_expo = jnp.where(tree_live, jnp.exp(tree_scores - row_peak[..., None]), 0.0)
        row_total = lax.optimization_barrier(jnp.sum(cache_expo, axis=-1)) + lax.optimization_barrier(jnp.sum(tree_expo, axis=-1))
        cache_weights = lax.optimization_barrier(cache_expo.astype(jnp.bfloat16)).astype(jnp.float32)
        tree_weights = lax.optimization_barrier(tree_expo.astype(jnp.bfloat16)).astype(jnp.float32)
        weighted = jnp.einsum('nhp,pc->nhc', cache_weights, cache_rows[:, :LAT])
        weighted = weighted + jnp.einsum('nhp,pc->nhc', tree_weights, tree_rows[:, :LAT])
        latent_out = weighted / row_total[..., None]
        return jnp.einsum('nhc,hcv->nhv', latent_out, value_weight, precision=lax.Precision.HIGHEST).astype(jnp.bfloat16)
    head_out = lax.map(per_slot, jnp.arange(SEQS, dtype=jnp.int32))
    flat_rows = head_out.reshape(SEQS * NODES, H * VD)
    attended = jnp.dot(flat_rows, out_proj, preferred_element_type=jnp.float32).astype(jnp.bfloat16)
    return attended.reshape(SEQS, NODES, D)
```

```python
import math

import jax
import jax.numpy as jnp
from jax import lax
from jax.experimental import pallas as pl
from jax.experimental.pallas import tpu as pltpu
from jax.sharding import PartitionSpec as P

MESH = pl.DeviceIdType.MESH
F32 = jnp.float32
BF16 = jnp.bfloat16
GROUPS = 2
DEAD = -1e30


def nt_dot(a, b):
    return lax.dot_general(a, b, (((1,), (1,)), ((), ())), preferred_element_type=F32)


def nn_dot(a, b):
    return jnp.dot(a, b, preferred_element_type=F32)


def permuted(source_of, value):
    rows = value.shape[0]
    r = lax.broadcasted_iota(jnp.int32, (rows, rows), 0)
    s = lax.broadcasted_iota(jnp.int32, (rows, rows), 1)
    select = jnp.where(source_of(r) == s, 1.0, 0.0).astype(BF16)
    return nn_dot(select, value).astype(BF16)


def kernel(
    cache_ref, length_ref, slot_ref, parents_ref, nope_ref, rope_ref, latent_ref, key_up_ref, value_up_ref, proj_ref,
    out_ref,
    raw, live, keys, nope, rope, tree_rows, key_up, value_up, proj, queries, heads, partial, sums,
    local_sem, raw_sem, live_sem, key_sem, a_sem, b_sem, sum_sem, send_sem,
):
    ctx, tp, dec = lax.axis_index("ctx"), lax.axis_index("tp"), lax.axis_index("dec")
    x, z_lo = dec // 2, dec % 2
    y, core = tp // 2, tp % 2
    z = ctx * 2 + z_lo
    nodes, head_count = 16, 16
    scale = 1.0 / math.sqrt(192.0)

    def at_x(dx, dz=0):
        xx, zz = (x + dx + 4) % 4, (z + dz + 8) % 8
        return (zz // 2, tp, xx * 2 + zz % 2)

    def at_tp(dy, other_core=False):
        core_there = 1 - core if other_core else core
        return (ctx, ((y + dy) % 4) * 2 + core_there, dec)

    def at_dec(k):
        return (ctx, tp, (dec + k) % 8)

    def at_ctx(k):
        return ((ctx + k) % 4, tp, dec)

    peers = [at_dec(k) for k in range(1, 8)]
    peers += [at_ctx(k) for k in range(1, 4)]
    peers += [at_tp(dy) for dy in (1, 2, 3)] + [at_tp(dy, True) for dy in range(4)]
    away = (z + 7 + 2 * z_lo) % 8
    peers.append((away // 2, tp, x * 2 + away % 2))

    started = []

    def send(src, dst, sem, device):
        copy = pltpu.make_async_remote_copy(
            src_ref=src, dst_ref=dst, send_sem=send_sem.at[len(started)], recv_sem=sem,
            device_id=device, device_id_type=MESH,
        )
        copy.start()
        started.append(copy)

    def arrived(dst, sem):
        pltpu.make_async_remote_copy(
            src_ref=dst, dst_ref=dst, send_sem=send_sem.at[0], recv_sem=sem,
            device_id=at_dec(1), device_id_type=MESH,
        ).wait_recv()

    loads = []

    def load(src, dst):
        copy = pltpu.make_async_copy(src, dst, local_sem.at[len(loads)])
        copy.start()
        loads.append(copy)
        return copy

    own_rows = cache_ref.at[pl.ds(pl.multiple_of(tp * 32, 32), 32)]
    load_raw = load(own_rows, raw.at[dec])
    load_nope = load(nope_ref.at[:, pl.ds(ctx * 2, 2)], nope)
    load_rope = load(rope_ref.at[:, pl.ds(ctx * 2, 2)], rope)
    load_tree = load(latent_ref, tree_rows)
    load_key_up = load(key_up_ref, key_up)
    load_value_up = load(value_up_ref, value_up)
    load_proj = load(proj_ref, proj)

    live[dec] = jnp.full((8, 128), length_ref[0], jnp.int32)

    barrier = pltpu.get_barrier_semaphore()
    for peer in peers:
        pl.semaphore_signal(barrier, inc=1, device_id=peer, device_id_type=MESH)
    pl.semaphore_wait(barrier, len(peers))

    for k in range(1, 8):
        send(live.at[dec], live.at[dec], live_sem.at[dec], at_dec(k))
        send(own_rows, raw.at[dec], raw_sem.at[dec], at_dec(k))

    j_at = lax.broadcasted_iota(jnp.int32, (64, 64), 0)
    i_at = lax.broadcasted_iota(jnp.int32, (64, 64), 1)
    closure = jnp.where((parents_ref[...] == j_at) | (i_at == j_at), 1.0, 0.0)
    for _ in range(6):
        closure = jnp.minimum(nn_dot(closure.astype(BF16), closure.astype(BF16)), 1.0)
    row = lax.broadcasted_iota(jnp.int32, (128, 64), 0) % 16
    own_node = lax.broadcasted_iota(jnp.int32, (128, 64), 1) == 8 * (row // 2) + 2 * ctx + row % 2
    on_path = nt_dot(jnp.where(own_node, 1.0, 0.0).astype(BF16), closure.astype(BF16))
    tree_bias = (on_path - 1.0) * 1e30

    def by_head(r):
        return (r % 16) * 16 + r // 16

    load_nope.wait()
    load_rope.wait()
    nope_rows = permuted(by_head, nope[...].reshape(256, 128))
    rope_rows = permuted(by_head, rope[...].reshape(256, 64))
    lane = lax.broadcasted_iota(jnp.int32, (256, 64), 1)
    queries[:, 512:640] = jnp.concatenate([rope_rows, jnp.where(lane == 0, 1.0, 0.0).astype(BF16)], axis=1)
    load_key_up.wait()
    for h in range(head_count):
        rows = slice(h * nodes, (h + 1) * nodes)
        queries[rows, 0:512] = nn_dot(nope_rows[rows], key_up[h]).astype(BF16)

    load_raw.wait()
    for k in range(1, 8):
        source = (dec + k) % 8
        arrived(live.at[source], live_sem.at[source])
        arrived(raw.at[source], raw_sem.at[source])
    wanted = slot_ref[dec]
    position = ctx * 256 + tp * 32 + lax.broadcasted_iota(jnp.int32, (32, 64), 0)
    first_lane = lax.broadcasted_iota(jnp.int32, (32, 64), 1) == 0
    dead = (position >= live[wanted][0:1, 0:64]) & first_lane
    keys[ctx * 8 + tp] = jnp.concatenate([raw[wanted], jnp.where(dead, DEAD, 0.0).astype(BF16)], axis=1)

    def pass_on(slot, device):
        send(keys.at[slot], keys.at[slot], key_sem.at[slot], device)

    own_slot = ctx * 8 + tp
    for k in (1, 3, 2):
        pass_on(own_slot, at_ctx(k))
    for k in (0, 1, 3, 2):
        slot = ((ctx + k) % 4) * 8 + tp
        if k:
            arrived(keys.at[slot], key_sem.at[slot])
        for dy in (1, 3, 2):
            pass_on(slot, at_tp(dy))
        pass_on(slot, at_tp(0, True))
    for k in (0, 1, 3, 2):
        for dy in (1, 3, 2):
            slot = ((ctx + k) % 4) * 8 + ((y + dy) % 4) * 2 + core
            arrived(keys.at[slot], key_sem.at[slot])
            pass_on(slot, at_tp(0, True))
    for k in (0, 1, 3, 2):
        for dy in (0, 1, 3, 2):
            slot = ((ctx + k) % 4) * 8 + ((y + dy) % 4) * 2 + 1 - core
            arrived(keys.at[slot], key_sem.at[slot])

    load_tree.wait()
    load_value_up.wait()

    group_heads = head_count // GROUPS
    group_rows = group_heads * nodes

    def attend(g):
        q = queries[g * group_rows : (g + 1) * group_rows, :]
        s = nt_dot(q, keys[...].reshape(1024, 640)) * scale
        s_tree = nt_dot(q[:, :576], tree_rows[...]) * scale + tree_bias[:group_rows]
        peak = jnp.maximum(jnp.max(s, axis=-1, keepdims=True), jnp.max(s_tree, axis=-1, keepdims=True))
        e = jnp.exp(s - peak)
        e_tree = jnp.exp(s_tree - peak)
        total = jnp.sum(e, axis=-1, keepdims=True) + jnp.sum(e_tree, axis=-1, keepdims=True)
        o = nn_dot(e.astype(BF16), keys[:, :, 0:512].reshape(1024, 512))
        o = o + nn_dot(e_tree.astype(BF16), tree_rows[:, 0:512])
        o = (o / total).astype(BF16)
        for h in range(group_heads):
            head = g * group_heads + h
            done = nn_dot(o[h * nodes : (h + 1) * nodes], value_up[head]).astype(BF16)
            heads[z * 4 + x, :, head * 128 : (head + 1) * 128] = done

    a_width = group_heads * 3 // 8 * 128
    b_width = group_heads * 128 - a_width

    def block(part, g, dx, dz):
        slot = ((z + dz + 8) % 8) * 4 + (x + dx + 4) % 4
        start = g * group_heads * 128 + (0 if part == 0 else a_width)
        ref = heads.at[slot, :, pl.ds(start, a_width if part == 0 else b_width)]
        return ref, (a_sem, b_sem)[part].at[g * 32 + slot]

    def relay(part, g, dx, dz, to_dx, to_dz):
        ref, sem = block(part, g, dx, dz)
        send(ref, ref, sem, at_x(to_dx, to_dz))

    def come(part, g, dx, dz):
        ref, sem = block(part, g, dx, dz)
        arrived(ref, sem)

    def reach(plus, far):
        return (4 if far else 3) if plus else (3 if far else 4)

    def along_z(part, g, dx, s, far):
        if s == 0:
            relay(part, g, dx, 0, 0, 1)
            relay(part, g, dx, 0, 0, -1)
            return
        for plus in (True, False):
            if s <= reach(plus, far):
                dz = -s if plus else s
                come(part, g, dx, dz)
                if s < reach(plus, far):
                    relay(part, g, dx, dz, 0, 1 if plus else -1)

    def steps(part, g, dx, s, far):
        return [(-s if plus else s) for plus in (True, False) if s <= reach(plus, far)]

    def launch(g):
        along_z(1, g, 0, 0, g % 2 == 0)
        for dx in (1, -1, 2):
            relay(0, g, 0, 0, dx, 0)
        relay(1, g, 0, 0, 1, 0)
        relay(1, g, 0, 0, -1, 0)
        along_z(0, g, 0, 0, True)

    def x_hop(g, dz):
        come(1, g, -1, dz)
        if dz % 2 == 0:
            relay(1, g, -1, dz, 1, 0)
        come(1, g, 1, dz)
        if dz % 2 == 1:
            relay(1, g, 1, dz, -1, 0)

    def step(g, s):
        far_b = g % 2 == 0
        if s == 1:
            for dx in (1, -1, 2):
                come(0, g, dx, 0)
                along_z(0, g, dx, 0, dx == 2)
        if s <= 4:
            along_z(1, g, 0, s, far_b)
            for dz in steps(1, g, 0, s, far_b):
                relay(1, g, 0, dz, 1, 0)
                relay(1, g, 0, dz, -1, 0)
        if s >= 2:
            for dx in (0, 1, -1, 2):
                along_z(0, g, dx, s - 1, dx in (0, 2))
        for dz in steps(1, g, 0, s - 1, far_b) if s > 1 else [0]:
            x_hop(g, dz)

    for g in range(GROUPS):
        attend(g)
        launch(g)
    for s in range(1, 6):
        for g in range(GROUPS):
            step(g, s)
    for s in range(5):
        for g in range(GROUPS):
            for dz in steps(1, g, 0, s, g % 2 == 0) if s else [0]:
                come(1, g, 2, dz)

    load_proj.wait()

    def by_target(r):
        j, rest = r // 16, r % 16
        return (rest // 2) * 16 + 2 * j + rest % 2

    for k in (0, 1, 3, 2):
        origin = (ctx + k) % 4
        rows = heads[pl.ds(origin * 8, 8)].reshape(128, 2048)
        product = nn_dot(rows, proj[...]).astype(BF16)
        partial[origin] = permuted(by_target, product).reshape(8, 16, 224)
        sums[origin, tp] = partial[origin, tp]
        for dy in range(4):
            for other in (False, True):
                if dy or other:
                    device = at_tp(dy, other)
                    send(partial.at[origin, device[1]], sums.at[origin, tp], sum_sem.at[origin * 8 + tp], device)
    totals = []
    for origin in range(4):
        for dy in range(4):
            for other in (False, True):
                if dy or other:
                    source = at_tp(dy, other)[1]
                    arrived(sums.at[origin, source], sum_sem.at[origin * 8 + source])
    for origin in range(4):
        total = jnp.zeros((16, 224), F32)
        for source in range(8):
            total = total + sums[origin, source].astype(F32)
        totals.append(total.astype(BF16))

    def by_slot(r):
        return ((r // 2) % 4) * 16 + ((r // 8) % 2) * 8 + (r // 16) * 2 + r % 2

    out_ref[...] = permuted(by_slot, jnp.concatenate(totals, axis=0))
    for copy in started:
        copy.wait_send()


SENDS = 448


def on_device(cache, lengths, slots, parents, nope, rope, latent_rows, key_up, value_up, proj):
    anywhere = pl.BlockSpec(memory_space=pl.ANY)
    in_vmem = pl.BlockSpec(memory_space=pltpu.VMEM)
    in_smem = pl.BlockSpec(memory_space=pltpu.SMEM)
    dma = pltpu.SemaphoreType.DMA
    out = pl.pallas_call(
        kernel,
        out_shape=jax.ShapeDtypeStruct((64, 224), BF16),
        in_specs=[anywhere, in_smem, in_smem, in_vmem] + [anywhere] * 6,
        out_specs=in_vmem,
        scratch_shapes=[
            pltpu.VMEM((8, 32, 576), BF16),
            pltpu.VMEM((8, 8, 128), jnp.int32),
            pltpu.VMEM((32, 32, 640), BF16),
            pltpu.VMEM((8, 2, 16, 128), BF16),
            pltpu.VMEM((8, 2, 16, 64), BF16),
            pltpu.VMEM((64, 576), BF16),
            pltpu.VMEM((16, 128, 512), BF16),
            pltpu.VMEM((16, 512, 128), BF16),
            pltpu.VMEM((2048, 224), BF16),
            pltpu.VMEM((256, 640), BF16),
            pltpu.VMEM((32, 16, 2048), BF16),
            pltpu.VMEM((4, 8, 16, 224), BF16),
            pltpu.VMEM((4, 8, 16, 224), BF16),
            dma((8,)), dma((8,)), dma((8,)), dma((32,)), dma((GROUPS * 32,)), dma((GROUPS * 32,)), dma((32,)),
            dma((SENDS,)),
        ],
        compiler_params=pltpu.CompilerParams(
            collective_id=0, has_side_effects=True, vmem_limit_bytes=48 * 1024 * 1024
        ),
        name="tree_attention",
    )(
        cache.reshape(cache.shape[1:]), lengths, slots, parents,
        nope.reshape(8, 8, 16, 128), rope.reshape(8, 8, 16, 64), latent_rows.reshape(latent_rows.shape[1:]),
        key_up, value_up, proj,
    )
    return out.reshape(8, 8, 224)


def solution(mesh):
    return jax.shard_map(
        on_device,
        mesh=mesh,
        in_specs=(
            P("dec", "ctx", None),
            P("dec"),
            P(),
            P("dec", None),
            P("dec", None, "tp", None),
            P("dec", None, "tp", None),
            P("dec", None, None),
            P("tp", None, None),
            P("tp", None, None),
            P("tp", ("ctx", "dec")),
        ),
        out_specs=P(None, "tp", ("ctx", "dec")),
        check_vma=False,
    )
```

```python
import math

import jax
import jax.numpy as jnp
from jax import lax
from jax.experimental import pallas as pl
from jax.experimental.pallas import tpu as pltpu
from jax.sharding import PartitionSpec as P

MESH = pl.DeviceIdType.MESH
F32 = jnp.float32
BF16 = jnp.bfloat16
GROUPS = 2
DEAD = -1e30


def nt_dot(a, b):
    return lax.dot_general(a, b, (((1,), (1,)), ((), ())), preferred_element_type=F32)


def nn_dot(a, b):
    return jnp.dot(a, b, preferred_element_type=F32)


def permuted(source_of, value):
    rows = value.shape[0]
    r = lax.broadcasted_iota(jnp.int32, (rows, rows), 0)
    s = lax.broadcasted_iota(jnp.int32, (rows, rows), 1)
    select = jnp.where(source_of(r) == s, 1.0, 0.0).astype(BF16)
    return nn_dot(select, value).astype(BF16)


def kernel(
    cache_ref, length_ref, slot_ref, parents_ref, nope_ref, rope_ref, latent_ref, key_up_ref, value_up_ref, proj_ref,
    out_ref,
    raw, live, keys, parents, nope, rope, tree_rows, key_up, value_up, proj, queries, heads, partial, sums,
    local_sem, raw_sem, live_sem, key_sem, a_sem, b_sem, sum_sem, send_sem,
):
    ctx, tp, dec = lax.axis_index("ctx"), lax.axis_index("tp"), lax.axis_index("dec")
    x, z_lo = dec // 2, dec % 2
    y, core = tp // 2, tp % 2
    z = ctx * 2 + z_lo
    nodes, head_count = 16, 16
    scale = 1.0 / math.sqrt(192.0)

    def at_x(dx, dz=0):
        xx, zz = (x + dx + 4) % 4, (z + dz + 8) % 8
        return (zz // 2, tp, xx * 2 + zz % 2)

    def at_tp(dy, other_core=False):
        core_there = 1 - core if other_core else core
        return (ctx, ((y + dy) % 4) * 2 + core_there, dec)

    def at_dec(k):
        return (ctx, tp, (dec + k) % 8)

    def at_ctx(k):
        return ((ctx + k) % 4, tp, dec)

    peers = [at_dec(k) for k in range(1, 8)]
    peers += [at_ctx(k) for k in range(1, 4)]
    peers += [at_tp(dy) for dy in (1, 2, 3)] + [at_tp(dy, True) for dy in range(4)]
    away = (z + 7 + 2 * z_lo) % 8
    peers.append((away // 2, tp, x * 2 + away % 2))

    started = []

    def send(src, dst, sem, device):
        copy = pltpu.make_async_remote_copy(
            src_ref=src, dst_ref=dst, send_sem=send_sem.at[len(started)], recv_sem=sem,
            device_id=device, device_id_type=MESH,
        )
        copy.start()
        started.append(copy)

    def arrived(dst, sem):
        pltpu.make_async_remote_copy(
            src_ref=dst, dst_ref=dst, send_sem=send_sem.at[0], recv_sem=sem,
            device_id=at_dec(1), device_id_type=MESH,
        ).wait_recv()

    loads = []

    def load(src, dst):
        copy = pltpu.make_async_copy(src, dst, local_sem.at[len(loads)])
        copy.start()
        loads.append(copy)
        return copy

    own_rows = cache_ref.at[pl.ds(pl.multiple_of(y * 144, 16), 144), pl.ds(pl.multiple_of(core * 128, 128), 128)]
    load_raw = load(own_rows, raw.at[dec])
    load_nope = load(nope_ref.at[:, pl.ds(ctx * 2, 2)], nope)
    load_rope = load(rope_ref.at[:, pl.ds(ctx * 2, 2)], rope)
    load_parents = load(parents_ref, parents)
    load_tree = load(latent_ref, tree_rows)
    load_key_up = load(key_up_ref, key_up)
    load_value_up = load(value_up_ref, value_up)
    load_proj = load(proj_ref, proj)

    live[dec] = jnp.full((8, 128), length_ref[0], jnp.int32)

    barrier = pltpu.get_barrier_semaphore()
    for peer in peers:
        pl.semaphore_signal(barrier, inc=1, device_id=peer, device_id_type=MESH)
    pl.semaphore_wait(barrier, len(peers))

    for k in range(1, 8):
        send(live.at[dec], live.at[dec], live_sem.at[dec], at_dec(k))
        send(own_rows, raw.at[dec], raw_sem.at[dec], at_dec(k))

    j_at = lax.broadcasted_iota(jnp.int32, (64, 64), 0)
    i_at = lax.broadcasted_iota(jnp.int32, (64, 64), 1)
    load_parents.wait()
    closure = jnp.where((parents[...] == j_at) | (i_at == j_at), 1.0, 0.0)
    for _ in range(6):
        closure = jnp.minimum(nn_dot(closure.astype(BF16), closure.astype(BF16)), 1.0)
    row = lax.broadcasted_iota(jnp.int32, (128, 64), 0) % 16
    own_node = lax.broadcasted_iota(jnp.int32, (128, 64), 1) == 8 * (row // 2) + 2 * ctx + row % 2
    on_path = nt_dot(jnp.where(own_node, 1.0, 0.0).astype(BF16), closure.astype(BF16))
    tree_bias = (on_path - 1.0) * 1e30

    def by_head(r):
        return (r % 16) * 16 + r // 16

    load_nope.wait()
    load_rope.wait()
    nope_rows = permuted(by_head, nope[...].reshape(256, 128))
    rope_rows = permuted(by_head, rope[...].reshape(256, 64))
    queries[:, 512:576] = rope_rows
    load_key_up.wait()
    for h in range(head_count):
        rows = slice(h * nodes, (h + 1) * nodes)
        queries[rows, 0:512] = nn_dot(nope_rows[rows], key_up[h]).astype(BF16)

    load_raw.wait()
    for k in range(1, 8):
        source = (dec + k) % 8
        arrived(live.at[source], live_sem.at[source])
        arrived(raw.at[source], raw_sem.at[source])
    wanted = slot_ref[dec]
    position = lax.broadcasted_iota(jnp.int32, (8, 128), 1)
    length = live[wanted]
    bias = jnp.concatenate(
        [jnp.where(position + start < length, 0.0, DEAD)[0:1] for start in range(0, 1024, 128)], axis=1
    )

    def key_part(c, t):
        rows = pl.ds(pl.multiple_of((t // 2) * 144, 16), 144)
        return keys.at[rows, pl.ds(pl.multiple_of(c * 256 + (t % 2) * 128, 128), 128)]

    key_part(ctx, tp)[...] = raw[wanted]

    def pass_on(k, t, device):
        c = (ctx + k) % 4
        send(key_part(c, t), key_part(c, t), key_sem.at[c * 8 + t], device)

    def come_key(k, t):
        c = (ctx + k) % 4
        arrived(key_part(c, t), key_sem.at[c * 8 + t])

    for k in (1, 3, 2):
        pass_on(0, tp, at_ctx(k))
    for k in (0, 1, 3, 2):
        if k:
            come_key(k, tp)
        for dy in (1, 3, 2):
            pass_on(k, tp, at_tp(dy))
        pass_on(k, tp, at_tp(0, True))
    for k in (0, 1, 3, 2):
        for dy in (1, 3, 2):
            come_key(k, at_tp(dy)[1])
            pass_on(k, at_tp(dy)[1], at_tp(0, True))
    for k in (0, 1, 3, 2):
        for dy in (0, 1, 3, 2):
            come_key(k, at_tp(dy, True)[1])

    load_tree.wait()
    load_value_up.wait()

    group_heads = head_count // GROUPS
    group_rows = group_heads * nodes

    def attend(g):
        q = queries[g * group_rows : (g + 1) * group_rows, :]
        s = nn_dot(q, keys[...]) * scale + bias
        s_tree = nt_dot(q, tree_rows[...]) * scale + tree_bias[:group_rows]
        peak = jnp.maximum(jnp.max(s, axis=-1, keepdims=True), jnp.max(s_tree, axis=-1, keepdims=True))
        e = jnp.exp(s - peak)
        e_tree = jnp.exp(s_tree - peak)
        total = jnp.sum(e, axis=-1, keepdims=True) + jnp.sum(e_tree, axis=-1, keepdims=True)
        o = nt_dot(e.astype(BF16), keys[0:512, :])
        o = o + nn_dot(e_tree.astype(BF16), tree_rows[:, 0:512])
        o = (o / total).astype(BF16)
        for h in range(group_heads):
            head = g * group_heads + h
            done = nn_dot(o[h * nodes : (h + 1) * nodes], value_up[head]).astype(BF16)
            heads[z * 4 + x, :, head * 128 : (head + 1) * 128] = done

    a_width = group_heads * 3 // 8 * 128
    b_width = group_heads * 128 - a_width

    def block(part, g, dx, dz):
        slot = ((z + dz + 8) % 8) * 4 + (x + dx + 4) % 4
        start = g * group_heads * 128 + (0 if part == 0 else a_width)
        ref = heads.at[slot, :, pl.ds(start, a_width if part == 0 else b_width)]
        return ref, (a_sem, b_sem)[part].at[g * 32 + slot]

    def relay(part, g, dx, dz, to_dx, to_dz):
        ref, sem = block(part, g, dx, dz)
        send(ref, ref, sem, at_x(to_dx, to_dz))

    def come(part, g, dx, dz):
        ref, sem = block(part, g, dx, dz)
        arrived(ref, sem)

    def reach(plus, far):
        return (4 if far else 3) if plus else (3 if far else 4)

    def along_z(part, g, dx, s, far):
        if s == 0:
            relay(part, g, dx, 0, 0, 1)
            relay(part, g, dx, 0, 0, -1)
            return
        for plus in (True, False):
            if s <= reach(plus, far):
                dz = -s if plus else s
                come(part, g, dx, dz)
                if s < reach(plus, far):
                    relay(part, g, dx, dz, 0, 1 if plus else -1)

    def steps(part, g, dx, s, far):
        return [(-s if plus else s) for plus in (True, False) if s <= reach(plus, far)]

    def launch(g):
        along_z(1, g, 0, 0, g % 2 == 0)
        for dx in (1, -1, 2):
            relay(0, g, 0, 0, dx, 0)
        relay(1, g, 0, 0, 1, 0)
        relay(1, g, 0, 0, -1, 0)
        along_z(0, g, 0, 0, True)

    def x_hop(g, dz):
        come(1, g, -1, dz)
        if dz % 2 == 0:
            relay(1, g, -1, dz, 1, 0)
        come(1, g, 1, dz)
        if dz % 2 == 1:
            relay(1, g, 1, dz, -1, 0)

    def step(g, s):
        far_b = g % 2 == 0
        if s == 1:
            for dx in (1, -1, 2):
                come(0, g, dx, 0)
                along_z(0, g, dx, 0, dx == 2)
        if s <= 4:
            along_z(1, g, 0, s, far_b)
            for dz in steps(1, g, 0, s, far_b):
                relay(1, g, 0, dz, 1, 0)
                relay(1, g, 0, dz, -1, 0)
        if s >= 2:
            for dx in (0, 1, -1, 2):
                along_z(0, g, dx, s - 1, dx in (0, 2))
        for dz in steps(1, g, 0, s - 1, far_b) if s > 1 else [0]:
            x_hop(g, dz)

    for g in range(GROUPS):
        attend(g)
        launch(g)
    for s in range(1, 6):
        for g in range(GROUPS):
            step(g, s)
    for s in range(5):
        for g in range(GROUPS):
            for dz in steps(1, g, 0, s, g % 2 == 0) if s else [0]:
                come(1, g, 2, dz)

    load_proj.wait()

    def by_target(r):
        j, rest = r // 16, r % 16
        return (rest // 2) * 16 + 2 * j + rest % 2

    for k in (0, 1, 3, 2):
        origin = (ctx + k) % 4
        rows = heads[pl.ds(origin * 8, 8)].reshape(128, 2048)
        product = nt_dot(rows, proj[...]).astype(BF16)
        partial[origin] = permuted(by_target, product).reshape(8, 16, 224)
        sums[origin, tp] = partial[origin, tp]
        for dy in range(4):
            for other in (False, True):
                if dy or other:
                    device = at_tp(dy, other)
                    send(partial.at[origin, device[1]], sums.at[origin, tp], sum_sem.at[origin * 8 + tp], device)
    totals = []
    for origin in range(4):
        for dy in range(4):
            for other in (False, True):
                if dy or other:
                    source = at_tp(dy, other)[1]
                    arrived(sums.at[origin, source], sum_sem.at[origin * 8 + source])
    for origin in range(4):
        total = jnp.zeros((16, 224), F32)
        for source in range(8):
            total = total + sums[origin, source].astype(F32)
        totals.append(total.astype(BF16))

    def by_slot(r):
        return ((r // 2) % 4) * 16 + ((r // 8) % 2) * 8 + (r // 16) * 2 + r % 2

    out_ref[...] = permuted(by_slot, jnp.concatenate(totals, axis=0))
    for copy in started:
        copy.wait_send()


SENDS = 448


def on_device(cache, lengths, slots, parents, nope, rope, latent_rows, key_up, value_up, proj):
    anywhere = pl.BlockSpec(memory_space=pl.ANY)
    in_vmem = pl.BlockSpec(memory_space=pltpu.VMEM)
    in_smem = pl.BlockSpec(memory_space=pltpu.SMEM)
    dma = pltpu.SemaphoreType.DMA
    out = pl.pallas_call(
        kernel,
        out_shape=jax.ShapeDtypeStruct((64, 224), BF16),
        in_specs=[anywhere, in_smem, in_smem] + [anywhere] * 7,
        out_specs=in_vmem,
        scratch_shapes=[
            pltpu.VMEM((8, 144, 128), BF16),
            pltpu.VMEM((8, 8, 128), jnp.int32),
            pltpu.VMEM((576, 1024), BF16),
            pltpu.VMEM((1, 64), jnp.int32),
            pltpu.VMEM((8, 2, 16, 128), BF16),
            pltpu.VMEM((8, 2, 16, 64), BF16),
            pltpu.VMEM((64, 576), BF16),
            pltpu.VMEM((16, 128, 512), BF16),
            pltpu.VMEM((16, 512, 128), BF16),
            pltpu.VMEM((224, 2048), BF16),
            pltpu.VMEM((256, 576), BF16),
            pltpu.VMEM((32, 16, 2048), BF16),
            pltpu.VMEM((4, 8, 16, 224), BF16),
            pltpu.VMEM((4, 8, 16, 224), BF16),
            dma((8,)), dma((8,)), dma((8,)), dma((32,)), dma((GROUPS * 32,)), dma((GROUPS * 32,)), dma((32,)),
            dma((SENDS,)),
        ],
        compiler_params=pltpu.CompilerParams(
            collective_id=0, has_side_effects=True, vmem_limit_bytes=58 * 1024 * 1024
        ),
        name="tree_attention",
    )(
        cache[0].T, lengths, slots, parents,
        nope.reshape(8, 8, 16, 128), rope.reshape(8, 8, 16, 64), latent_rows.reshape(latent_rows.shape[1:]),
        key_up, value_up, proj.T,
    )
    return out.reshape(8, 8, 224)


def solution(mesh):
    return jax.shard_map(
        on_device,
        mesh=mesh,
        in_specs=(
            P("dec", "ctx", None),
            P("dec"),
            P(),
            P("dec", None),
            P("dec", None, "tp", None),
            P("dec", None, "tp", None),
            P("dec", None, None),
            P("tp", None, None),
            P("tp", None, None),
            P("tp", ("ctx", "dec")),
        ),
        out_specs=P(None, "tp", ("ctx", "dec")),
        check_vma=False,
    )
```

```python
import math

import jax
import jax.numpy as jnp
from jax import lax
from jax.experimental import pallas as pl
from jax.experimental.pallas import tpu as pltpu
from jax.sharding import PartitionSpec as P

MESH = pl.DeviceIdType.MESH
F32 = jnp.float32
BF16 = jnp.bfloat16
GROUPS = 2
DEAD = -1e30
OFFSETS = [0, -1, 1, -2, 2, -3, 3, -4, 4]
HEAD_SEMS = ["a", "near", "far"]
HEAD_SEMS += [f"{part}{dz}" for part in ("a", "b") for dz in OFFSETS[1:]]
HEAD_SEMS += [f"x{side}{dz}" for side in "-+" for dz in OFFSETS]


def nt_dot(a, b):
    return lax.dot_general(a, b, (((1,), (1,)), ((), ())), preferred_element_type=F32)


def nn_dot(a, b):
    return jnp.dot(a, b, preferred_element_type=F32)


def permuted(source_of, value):
    rows = value.shape[0]
    r = lax.broadcasted_iota(jnp.int32, (rows, rows), 0)
    s = lax.broadcasted_iota(jnp.int32, (rows, rows), 1)
    select = jnp.where(source_of(r) == s, 1.0, 0.0).astype(BF16)
    return nn_dot(select, value).astype(BF16)


def kernel(
    cache_ref, length_ref, slot_ref, parents_ref, nope_ref, rope_ref, latent_ref, key_up_ref, value_up_ref, proj_ref,
    out_ref,
    raw, live, keys, parents, nope, rope, tree_rows, key_up, value_up, proj, queries, heads, partial, sums,
    local_sem, raw_sem, key_sem, head_sem, send_sem,
):
    ctx, tp, dec = lax.axis_index("ctx"), lax.axis_index("tp"), lax.axis_index("dec")
    x, z_lo = dec // 2, dec % 2
    y, core = tp // 2, tp % 2
    z = ctx * 2 + z_lo
    nodes, head_count = 16, 16
    scale = 1.0 / math.sqrt(192.0)

    def at_x(dx, dz=0):
        xx, zz = (x + dx + 4) % 4, (z + dz + 8) % 8
        return (zz // 2, tp, xx * 2 + zz % 2)

    def at_tp(dy, other_core=False):
        core_there = 1 - core if other_core else core
        return (ctx, ((y + dy) % 4) * 2 + core_there, dec)

    def at_dec(k):
        return (ctx, tp, (dec + k) % 8)

    def at_ctx(k):
        return ((ctx + k) % 4, tp, dec)

    peers = [at_dec(k) for k in range(1, 8)]
    peers += [at_ctx(k) for k in range(1, 4)]
    peers += [at_tp(dy) for dy in (1, 2, 3)] + [at_tp(dy, True) for dy in range(4)]
    away = (z + 7 + 2 * z_lo) % 8
    peers.append((away // 2, tp, x * 2 + away % 2))

    LIVE, RAW, KEYS, HEADS, SUMS = range(5)

    def described(src, dst, kind, sem, device):
        return pltpu.make_async_remote_copy(
            src_ref=src, dst_ref=dst, send_sem=send_sem.at[kind], recv_sem=sem,
            device_id=device, device_id_type=MESH,
        )

    def send(kind, ref, dst, sem, device):
        described(ref, dst, kind, sem, device).start()

    def arrived(dst, sem):
        described(dst, dst, 0, sem, at_dec(1)).wait_recv()

    def all_sent(kind, as_many_bytes):
        described(as_many_bytes, as_many_bytes, kind, raw_sem.at[0], at_dec(1)).wait_send()

    loads = []

    def load(src, dst):
        copy = pltpu.make_async_copy(src, dst, local_sem.at[len(loads)])
        copy.start()
        loads.append(copy)
        return copy

    own_rows = cache_ref.at[pl.ds(pl.multiple_of(y * 144, 16), 144), pl.ds(pl.multiple_of(core * 128, 128), 128)]
    load_raw = load(own_rows, raw.at[dec])
    load_nope = load(nope_ref.at[:, pl.ds(ctx * 2, 2)], nope)
    load_rope = load(rope_ref.at[:, pl.ds(ctx * 2, 2)], rope)
    load_parents = load(parents_ref, parents)
    load_tree = load(latent_ref, tree_rows)
    load_key_up = load(key_up_ref, key_up)
    load_value_up = load(value_up_ref, value_up)
    load_proj = load(proj_ref, proj)

    live[dec] = jnp.full((8, 128), length_ref[0], jnp.int32)

    barrier = pltpu.get_barrier_semaphore()
    for peer in peers:
        pl.semaphore_signal(barrier, inc=1, device_id=peer, device_id_type=MESH)
    pl.semaphore_wait(barrier, len(peers))

    for k in range(1, 8):
        send(LIVE, live.at[dec], live.at[dec], raw_sem.at[1], at_dec(k))
        send(RAW, own_rows, raw.at[dec], raw_sem.at[0], at_dec(k))

    j_at = lax.broadcasted_iota(jnp.int32, (64, 64), 0)
    i_at = lax.broadcasted_iota(jnp.int32, (64, 64), 1)
    load_parents.wait()
    closure = jnp.where((parents[...] == j_at) | (i_at == j_at), 1.0, 0.0)
    for _ in range(6):
        closure = jnp.minimum(nn_dot(closure.astype(BF16), closure.astype(BF16)), 1.0)
    row = lax.broadcasted_iota(jnp.int32, (128, 64), 0) % 16
    own_node = lax.broadcasted_iota(jnp.int32, (128, 64), 1) == 8 * (row // 2) + 2 * ctx + row % 2
    on_path = nt_dot(jnp.where(own_node, 1.0, 0.0).astype(BF16), closure.astype(BF16))
    tree_bias = (on_path - 1.0) * 1e30

    def by_head(r):
        return (r % 16) * 16 + r // 16

    load_nope.wait()
    load_rope.wait()
    nope_rows = permuted(by_head, nope[...].reshape(256, 128))
    rope_rows = permuted(by_head, rope[...].reshape(256, 64))
    queries[:, 512:576] = rope_rows
    load_key_up.wait()
    for h in range(head_count):
        rows = slice(h * nodes, (h + 1) * nodes)
        queries[rows, 0:512] = nn_dot(nope_rows[rows], key_up[h]).astype(BF16)

    load_raw.wait()
    arrived(live.at[pl.ds(0, 7)], raw_sem.at[1])
    arrived(raw.at[pl.ds(0, 7)], raw_sem.at[0])
    wanted = slot_ref[dec]
    position = lax.broadcasted_iota(jnp.int32, (8, 128), 1)
    length = live[wanted]
    bias = jnp.concatenate(
        [jnp.where(position + start < length, 0.0, DEAD)[0:1] for start in range(0, 1024, 128)], axis=1
    )

    def key_part(c, t):
        rows = pl.ds(pl.multiple_of((t // 2) * 144, 16), 144)
        return keys.at[rows, pl.ds(pl.multiple_of(c * 256 + (t % 2) * 128, 128), 128)]

    key_part(ctx, tp)[...] = raw[wanted]

    def key_piece(k, t, sem, device):
        c = (ctx + k) % 4
        send(KEYS, key_part(c, t), key_part(c, t), key_sem.at[sem], device)

    def come_key(k, t, sem):
        arrived(key_part((ctx + k) % 4, t), key_sem.at[sem])

    for k in (1, 3, 2):
        key_piece(0, tp, (4 - k) * 4, at_ctx(k))
    for k in (0, 1, 3, 2):
        if k:
            come_key(k, tp, k * 4)
        for dy in (1, 3, 2):
            key_piece(k, tp, k * 4 + 4 - dy, at_tp(dy))
        key_piece(k, tp, 0, at_tp(0, True))
    for k in (0, 1, 3, 2):
        for dy in (1, 3, 2):
            come_key(k, at_tp(dy)[1], k * 4 + dy)
            key_piece(k, at_tp(dy)[1], 0, at_tp(0, True))
    arrived(keys.at[pl.ds(0, 288)], key_sem.at[0])

    load_tree.wait()
    load_value_up.wait()

    group_heads = head_count // GROUPS
    group_rows = group_heads * nodes

    def attend(g):
        q = queries[g * group_rows : (g + 1) * group_rows, :]
        s = nn_dot(q, keys[...]) * scale + bias
        s_tree = nt_dot(q, tree_rows[...]) * scale + tree_bias[:group_rows]
        peak = jnp.maximum(jnp.max(s, axis=-1, keepdims=True), jnp.max(s_tree, axis=-1, keepdims=True))
        e = jnp.exp(s - peak)
        e_tree = jnp.exp(s_tree - peak)
        total = jnp.sum(e, axis=-1, keepdims=True) + jnp.sum(e_tree, axis=-1, keepdims=True)
        o = nt_dot(e.astype(BF16), keys[0:512, :])
        o = o + nn_dot(e_tree.astype(BF16), tree_rows[:, 0:512])
        o = (o / total).astype(BF16)
        for h in range(group_heads):
            head = g * group_heads + h
            done = nn_dot(o[h * nodes : (h + 1) * nodes], value_up[head]).astype(BF16)
            heads[z * 4 + x, :, head * 128 : (head + 1) * 128] = done

    a_width = group_heads * 3 // 8 * 128
    b_width = group_heads * 128 - a_width

    A, B = 0, 1

    def columns(part, g):
        start = g * group_heads * 128 + (0 if part == A else a_width)
        return pl.ds(start, a_width if part == A else b_width)

    def block(part, g, dx, dz):
        return heads.at[((z + dz + 8) % 8) * 4 + (x + dx + 4) % 4, :, columns(part, g)]

    def column_blocks(g, dz, first, count):
        return heads.at[pl.ds(((z + dz + 8) % 8) * 4 + first, count), :, columns(A, g)]

    def sem_of(g, name):
        return head_sem.at[g * len(HEAD_SEMS) + HEAD_SEMS.index(name)]

    def go(ref, g, name, dx, dz):
        send(HEADS, ref, ref, sem_of(g, name), at_x(dx, dz))

    def far_side(part, g):
        return 1 if (g % 2 == 0) == (part == B) else -1

    def sides(g, s):
        return (-s, s) if s < 4 else ((-4,) if far_side(B, g) == 1 else (4,))

    def launch(g):
        own = block(B, g, 0, 0)
        go(own, g, "b-1", 0, 1)
        go(own, g, "b1", 0, -1)
        for dx in (1, -1, 2):
            go(block(A, g, 0, 0), g, "a", dx, 0)
        go(own, g, "x-0", 1, 0)
        go(own, g, "x+0", -1, 0)

    def a_launch(g):
        arrived(heads.at[pl.ds(0, 3), :, columns(A, g)], sem_of(g, "a"))
        whole = column_blocks(g, 0, 0, 4)
        go(whole, g, "a-1", 0, 1)
        go(whole, g, "a1", 0, -1)

    def b_step(g, s):
        for dz in sides(g, s):
            ref = block(B, g, 0, dz)
            arrived(ref, sem_of(g, f"b{dz}"))
            onward = 1 if dz < 0 else -1
            if s < 3 or (s == 3 and onward == far_side(B, g)):
                go(ref, g, f"b{dz - onward}", 0, onward)
            go(ref, g, f"x-{dz}", 1, 0)
            go(ref, g, f"x+{dz}", -1, 0)

    def a_step(g, s):
        if s < 4:
            for dz in (-s, s):
                onward = 1 if dz < 0 else -1
                arrived(column_blocks(g, dz, 0, 4), sem_of(g, f"a{dz}"))
                if s < 3:
                    go(column_blocks(g, dz, 0, 4), g, f"a{dz - onward}", 0, onward)
                else:
                    go(column_blocks(g, dz, 0 if onward == 1 else 2, 2), g, f"a{dz - onward}", 0, onward)
        else:
            for dz in (-4, 4):
                arrived(column_blocks(g, dz, 0 if dz < 0 else 2, 2), sem_of(g, f"a{dz}"))

    def x_step(g, s):
        for dz in sides(g, s) if s else (0,):
            from_left = s == 0 or (dz < 0 if s < 4 else g % 2 == 0)
            for dx in (-1, 1):
                ref = block(B, g, dx, dz)
                arrived(ref, sem_of(g, f"x{'-' if dx < 0 else '+'}{dz}"))
                if (dx < 0) == from_left:
                    go(ref, g, "near" if s < 2 else "far", -dx, 0)

    def project(k):
        origin = (ctx + k) % 4
        rows = heads[pl.ds(origin * 8, 8)].reshape(128, 2048)
        product = nt_dot(rows, proj[...]).astype(BF16)
        partial[origin] = permuted(by_target, product).reshape(8, 16, 224)
        sums[origin, tp] = partial[origin, tp]
        for dy in (2, 1, 3, 0):
            for other in (False, True):
                if dy or other:
                    device = at_tp(dy, other)
                    send(SUMS, partial.at[origin, device[1]], sums.at[origin, tp], raw_sem.at[2], device)

    def by_target(r):
        j, rest = r // 16, r % 16
        return (rest // 2) * 16 + 2 * j + rest % 2

    groups = range(GROUPS)
    for g in groups:
        attend(g)
        launch(g)
    for g in groups:
        a_launch(g)
    load_proj.wait()
    for s in range(1, 6):
        if s < 5:
            for g in groups:
                b_step(g, s)
        if s > 1:
            for g in groups:
                a_step(g, s - 1)
        for g in groups:
            x_step(g, s - 1)
        if s == 4:
            for g in groups:
                arrived(heads.at[pl.ds(0, 3), :, columns(B, g)], sem_of(g, "near"))
            project(0)
    for g in groups:
        arrived(heads.at[pl.ds(0, 5), :, columns(B, g)], sem_of(g, "far"))
    for k in (1, 3, 2):
        project(k)
    every = sums.reshape(32, 16, 224)
    arrived(every.at[pl.ds(0, 28)], raw_sem.at[2])
    totals = []
    for origin in range(4):
        total = jnp.zeros((16, 224), F32)
        for source in range(8):
            total = total + sums[origin, source].astype(F32)
        totals.append(total.astype(BF16))

    def by_slot(r):
        return ((r // 2) % 4) * 16 + ((r // 8) % 2) * 8 + (r // 16) * 2 + r % 2

    out_ref[...] = permuted(by_slot, jnp.concatenate(totals, axis=0))
    all_sent(LIVE, live.at[pl.ds(0, 7)])
    all_sent(RAW, raw.at[pl.ds(0, 7)])
    all_sent(KEYS, value_up.reshape(8192, 128).at[pl.ds(0, 31 * 144)])
    all_sent(HEADS, heads.at[pl.ds(0, 31)])
    all_sent(SUMS, every.at[pl.ds(0, 28)])


def on_device(cache, lengths, slots, parents, nope, rope, latent_rows, key_up, value_up, proj):
    anywhere = pl.BlockSpec(memory_space=pl.ANY)
    in_vmem = pl.BlockSpec(memory_space=pltpu.VMEM)
    in_smem = pl.BlockSpec(memory_space=pltpu.SMEM)
    dma = pltpu.SemaphoreType.DMA
    out = pl.pallas_call(
        kernel,
        out_shape=jax.ShapeDtypeStruct((64, 224), BF16),
        in_specs=[anywhere, in_smem, in_smem] + [anywhere] * 7,
        out_specs=in_vmem,
        scratch_shapes=[
            pltpu.VMEM((8, 144, 128), BF16),
            pltpu.VMEM((8, 8, 128), jnp.int32),
            pltpu.VMEM((576, 1024), BF16),
            pltpu.VMEM((1, 64), jnp.int32),
            pltpu.VMEM((8, 2, 16, 128), BF16),
            pltpu.VMEM((8, 2, 16, 64), BF16),
            pltpu.VMEM((64, 576), BF16),
            pltpu.VMEM((16, 128, 512), BF16),
            pltpu.VMEM((16, 512, 128), BF16),
            pltpu.VMEM((224, 2048), BF16),
            pltpu.VMEM((256, 576), BF16),
            pltpu.VMEM((32, 16, 2048), BF16),
            pltpu.VMEM((4, 8, 16, 224), BF16),
            pltpu.VMEM((4, 8, 16, 224), BF16),
            dma((8,)), dma((3,)), dma((16,)), dma((GROUPS * len(HEAD_SEMS),)), dma((5,)),
        ],
        compiler_params=pltpu.CompilerParams(
            collective_id=0, has_side_effects=True, vmem_limit_bytes=58 * 1024 * 1024
        ),
        name="tree_attention",
    )(
        cache[0].T, lengths, slots, parents,
        nope.reshape(8, 8, 16, 128), rope.reshape(8, 8, 16, 64), latent_rows.reshape(latent_rows.shape[1:]),
        key_up, value_up, proj.T,
    )
    return out.reshape(8, 8, 224)


def solution(mesh):
    return jax.shard_map(
        on_device,
        mesh=mesh,
        in_specs=(
            P("dec", "ctx", None),
            P("dec"),
            P(),
            P("dec", None),
            P("dec", None, "tp", None),
            P("dec", None, "tp", None),
            P("dec", None, None),
            P("tp", None, None),
            P("tp", None, None),
            P("tp", ("ctx", "dec")),
        ),
        out_specs=P(None, "tp", ("ctx", "dec")),
        check_vma=False,
    )
```

```python
import math

import jax
import jax.numpy as jnp
from jax import lax
from jax.experimental import pallas as pl
from jax.experimental.pallas import tpu as pltpu
from jax.sharding import PartitionSpec as P

MESH = pl.DeviceIdType.MESH
F32 = jnp.float32
BF16 = jnp.bfloat16
GROUPS = 2
DEAD = -1e30
OFFSETS = [0, -1, 1, -2, 2, -3, 3, -4, 4]
HEAD_SEMS = ["a", "near", "mid", "far"]
HEAD_SEMS += [f"{part}{dz}" for part in ("a", "b") for dz in OFFSETS[1:]]
HEAD_SEMS += [f"x{side}{dz}" for side in "-+" for dz in OFFSETS]

ORDER = [
    ("L", 0), ("L", 1), ("b", 0, -1), ("b", 0, 1), ("x", 0, -1, 0), ("a", 0), ("x", 0, 1, 0), ("b", 1, -1),
    ("b", 1, 1), ("x", 1, 1, 0), ("a", 1), ("x", 1, -1, 0), ("b", 0, -2), ("x", 0, 1, -1), ("b", 0, 2),
    ("x", 0, -1, -1), ("x", 0, 1, 1), ("x", 0, -1, 1), ("A", 0, -1), ("A", 0, 1), ("x", 1, -1, -1), ("x", 1, 1, -1),
    ("b", 1, -2), ("b", 1, 2), ("x", 1, -1, 1), ("x", 1, 1, 1), ("x", 0, -1, -2), ("A", 1, -1), ("A", 1, 1),
    ("x", 0, 1, -2), ("x", 0, -1, 2), ("b", 0, -3), ("b", 0, 3), ("x", 0, 1, 2), ("b", 0, -4), ("x", 1, 1, -2),
    ("A", 0, 2), ("x", 1, -1, -2), ("x", 1, 1, 2), ("b", 1, 3), ("x", 1, -1, 2), ("A", 0, -2), ("b", 1, -3),
    ("x", 0, 1, -3), ("x", 0, -1, -3), ("b", 1, 4), ("x", 0, 1, 3), ("x", 0, -1, 3), ("A", 1, -2), ("x", 0, -1, -4),
    ("A", 1, 2), ("x", 0, 1, -4), ("P", 0), ("x", 1, -1, 3), ("A", 0, 3), ("x", 1, 1, 3), ("x", 1, -1, -3), ("A", 0, -3),
    ("x", 1, 1, -3), ("x", 1, 1, 4), ("x", 1, -1, 4), ("A", 0, 4), ("A", 0, -4), ("A", 1, 3), ("A", 1, -3), ("P", 1),
    ("A", 1, 4), ("A", 1, -4),
]


def nt_dot(a, b):
    return lax.dot_general(a, b, (((1,), (1,)), ((), ())), preferred_element_type=F32)


def nn_dot(a, b):
    return jnp.dot(a, b, preferred_element_type=F32)


def permuted(source_of, value):
    rows = value.shape[0]
    r = lax.broadcasted_iota(jnp.int32, (rows, rows), 0)
    s = lax.broadcasted_iota(jnp.int32, (rows, rows), 1)
    select = jnp.where(source_of(r) == s, 1.0, 0.0).astype(BF16)
    return nn_dot(select, value).astype(BF16)


def kernel(
    cache_ref, length_ref, slot_ref, parents_ref, nope_ref, rope_ref, latent_ref, key_up_ref, value_up_ref, proj_ref,
    out_ref,
    raw, live, keys, parents, nope, rope, tree_rows, key_up, value_up, proj, queries, heads, partial, sums,
    local_sem, raw_sem, key_sem, head_sem, send_sem,
):
    ctx, tp, dec = lax.axis_index("ctx"), lax.axis_index("tp"), lax.axis_index("dec")
    x, z_lo = dec // 2, dec % 2
    y, core = tp // 2, tp % 2
    z = ctx * 2 + z_lo
    nodes, head_count = 16, 16
    scale = 1.0 / math.sqrt(192.0)

    def at_x(dx, dz=0):
        xx, zz = (x + dx + 4) % 4, (z + dz + 8) % 8
        return (zz // 2, tp, xx * 2 + zz % 2)

    def at_tp(dy, other_core=False):
        core_there = 1 - core if other_core else core
        return (ctx, ((y + dy) % 4) * 2 + core_there, dec)

    def at_dec(k):
        return (ctx, tp, (dec + k) % 8)

    def at_ctx(k):
        return ((ctx + k) % 4, tp, dec)

    peers = [at_dec(k) for k in range(1, 8)]
    peers += [at_ctx(k) for k in range(1, 4)]
    peers += [at_tp(dy) for dy in (1, 2, 3)] + [at_tp(dy, True) for dy in range(4)]
    away = (z + 7 + 2 * z_lo) % 8
    peers.append((away // 2, tp, x * 2 + away % 2))

    LIVE, RAW, KEYS, HEADS, SUMS = range(5)

    def described(src, dst, kind, sem, device):
        return pltpu.make_async_remote_copy(
            src_ref=src, dst_ref=dst, send_sem=send_sem.at[kind], recv_sem=sem,
            device_id=device, device_id_type=MESH,
        )

    def send(kind, ref, dst, sem, device):
        described(ref, dst, kind, sem, device).start()

    def arrived(dst, sem):
        described(dst, dst, 0, sem, at_dec(1)).wait_recv()

    def all_sent(kind, as_many_bytes):
        described(as_many_bytes, as_many_bytes, kind, raw_sem.at[0], at_dec(1)).wait_send()

    loads = []

    def load(src, dst):
        copy = pltpu.make_async_copy(src, dst, local_sem.at[len(loads)])
        copy.start()
        loads.append(copy)
        return copy

    own_rows = cache_ref.at[pl.ds(pl.multiple_of(y * 144, 16), 144), pl.ds(pl.multiple_of(core * 128, 128), 128)]
    load_raw = load(own_rows, raw.at[dec])
    load_nope = load(nope_ref.at[:, pl.ds(ctx * 2, 2)], nope)
    load_rope = load(rope_ref.at[:, pl.ds(ctx * 2, 2)], rope)
    load_parents = load(parents_ref, parents)
    load_tree = load(latent_ref, tree_rows)
    load_key_up = load(key_up_ref, key_up)
    load_value_up = load(value_up_ref, value_up)
    load_proj = load(proj_ref, proj)

    live[dec] = jnp.full((8, 128), length_ref[0], jnp.int32)

    barrier = pltpu.get_barrier_semaphore()
    for peer in peers:
        pl.semaphore_signal(barrier, inc=1, device_id=peer, device_id_type=MESH)
    pl.semaphore_wait(barrier, len(peers))

    for k in range(1, 8):
        send(LIVE, live.at[dec], live.at[dec], raw_sem.at[1], at_dec(k))
        send(RAW, own_rows, raw.at[dec], raw_sem.at[0], at_dec(k))

    j_at = lax.broadcasted_iota(jnp.int32, (64, 64), 0)
    i_at = lax.broadcasted_iota(jnp.int32, (64, 64), 1)
    load_parents.wait()
    closure = jnp.where((parents[...] == j_at) | (i_at == j_at), 1.0, 0.0)
    for _ in range(6):
        closure = jnp.minimum(nn_dot(closure.astype(BF16), closure.astype(BF16)), 1.0)
    row = lax.broadcasted_iota(jnp.int32, (128, 64), 0) % 16
    own_node = lax.broadcasted_iota(jnp.int32, (128, 64), 1) == 8 * (row // 2) + 2 * ctx + row % 2
    on_path = nt_dot(jnp.where(own_node, 1.0, 0.0).astype(BF16), closure.astype(BF16))
    tree_bias = (on_path - 1.0) * 1e30

    def by_head(r):
        return (r % 16) * 16 + r // 16

    load_nope.wait()
    load_rope.wait()
    nope_rows = permuted(by_head, nope[...].reshape(256, 128))
    rope_rows = permuted(by_head, rope[...].reshape(256, 64))
    queries[:, 512:576] = rope_rows
    load_key_up.wait()
    for h in range(head_count):
        rows = slice(h * nodes, (h + 1) * nodes)
        queries[rows, 0:512] = nn_dot(nope_rows[rows], key_up[h]).astype(BF16)

    load_raw.wait()
    arrived(live.at[pl.ds(0, 7)], raw_sem.at[1])
    arrived(raw.at[pl.ds(0, 7)], raw_sem.at[0])
    wanted = slot_ref[dec]
    position = lax.broadcasted_iota(jnp.int32, (8, 128), 1)
    length = live[wanted]
    bias = jnp.concatenate(
        [jnp.where(position + start < length, 0.0, DEAD)[0:1] for start in range(0, 1024, 128)], axis=1
    )

    def key_part(c, t):
        rows = pl.ds(pl.multiple_of((t // 2) * 144, 16), 144)
        return keys.at[rows, pl.ds(pl.multiple_of(c * 256 + (t % 2) * 128, 128), 128)]

    key_part(ctx, tp)[...] = raw[wanted]

    def key_piece(k, t, sem, device):
        c = (ctx + k) % 4
        send(KEYS, key_part(c, t), key_part(c, t), key_sem.at[sem], device)

    def come_key(k, t, sem):
        arrived(key_part((ctx + k) % 4, t), key_sem.at[sem])

    for k in (1, 3, 2):
        key_piece(0, tp, (4 - k) * 4, at_ctx(k))
    def along_y(k):
        if k:
            come_key(k, tp, k * 4)
        for dy in (1, 3, 2):
            key_piece(k, tp, k * 4 + 4 - dy, at_tp(dy))
        key_piece(k, tp, 0, at_tp(0, True))

    def to_other_core(k):
        for dy in (1, 3, 2):
            come_key(k, at_tp(dy)[1], k * 4 + dy)
            key_piece(k, at_tp(dy)[1], 0, at_tp(0, True))

    along_y(0)
    along_y(1)
    along_y(3)
    to_other_core(0)
    along_y(2)
    for k in (1, 3, 2):
        to_other_core(k)
    arrived(keys.at[pl.ds(0, 288)], key_sem.at[0])

    load_tree.wait()
    load_value_up.wait()

    group_heads = head_count // GROUPS
    group_rows = group_heads * nodes

    def attend(g):
        q = queries[g * group_rows : (g + 1) * group_rows, :]
        s = nn_dot(q, keys[...]) * scale + bias
        s_tree = nt_dot(q, tree_rows[...]) * scale + tree_bias[:group_rows]
        peak = jnp.maximum(jnp.max(s, axis=-1, keepdims=True), jnp.max(s_tree, axis=-1, keepdims=True))
        e = jnp.exp(s - peak)
        e_tree = jnp.exp(s_tree - peak)
        total = jnp.sum(e, axis=-1, keepdims=True) + jnp.sum(e_tree, axis=-1, keepdims=True)
        o = nt_dot(e.astype(BF16), keys[0:512, :])
        o = o + nn_dot(e_tree.astype(BF16), tree_rows[:, 0:512])
        o = (o / total).astype(BF16)
        for h in range(group_heads):
            head = g * group_heads + h
            done = nn_dot(o[h * nodes : (h + 1) * nodes], value_up[head]).astype(BF16)
            heads[z * 4 + x, :, head * 128 : (head + 1) * 128] = done

    a_width = group_heads * 3 // 8 * 128
    b_width = group_heads * 128 - a_width

    A, B = 0, 1

    def columns(part, g):
        start = g * group_heads * 128 + (0 if part == A else a_width)
        return pl.ds(start, a_width if part == A else b_width)

    def block(part, g, dx, dz):
        return heads.at[((z + dz + 8) % 8) * 4 + (x + dx + 4) % 4, :, columns(part, g)]

    def column_blocks(g, dz, first, count):
        return heads.at[pl.ds(((z + dz + 8) % 8) * 4 + first, count), :, columns(A, g)]

    def sem_of(g, name):
        return head_sem.at[g * len(HEAD_SEMS) + HEAD_SEMS.index(name)]

    def go(ref, g, name, dx, dz):
        send(HEADS, ref, ref, sem_of(g, name), at_x(dx, dz))

    def far_side(part, g):
        return 1 if (g % 2 == 0) == (part == B) else -1

    def launch(g):
        own = block(B, g, 0, 0)
        go(own, g, "b-1", 0, 1)
        go(own, g, "b1", 0, -1)
        for dx in (1, -1, 2):
            go(block(A, g, 0, 0), g, "a", dx, 0)
        go(own, g, "x-0", 1, 0)
        go(own, g, "x+0", -1, 0)

    def a_launch(g):
        arrived(heads.at[pl.ds(0, 3), :, columns(A, g)], sem_of(g, "a"))
        whole = column_blocks(g, 0, 0, 4)
        go(whole, g, "a-1", 0, 1)
        go(whole, g, "a1", 0, -1)

    def b_step(g, dz):
        ref = block(B, g, 0, dz)
        arrived(ref, sem_of(g, f"b{dz}"))
        onward = 1 if dz < 0 else -1
        if abs(dz) <= 2:
            go(ref, g, f"b{dz - onward}", 0, onward)
        if abs(dz) == 2 and onward == far_side(B, g):
            go(ref, g, f"b{dz - 2 * onward}", 0, 2 * onward)
        go(ref, g, f"x-{dz}", 1, 0)
        go(ref, g, f"x+{dz}", -1, 0)

    def a_step(g, dz):
        onward = 1 if dz < 0 else -1
        half = 0 if onward == 1 else 2
        if abs(dz) == 4:
            arrived(column_blocks(g, dz, half, 2), sem_of(g, f"a{dz}"))
            return
        whole = column_blocks(g, dz, 0, 4)
        arrived(whole, sem_of(g, f"a{dz}"))
        if abs(dz) <= 2:
            go(whole, g, f"a{dz - onward}", 0, onward)
        if abs(dz) == 2:
            go(column_blocks(g, dz, half, 2), g, f"a{dz - 2 * onward}", 0, 2 * onward)

    def x_step(g, dx, dz):
        ref = block(B, g, dx, dz)
        arrived(ref, sem_of(g, f"x{'-' if dx < 0 else '+'}{dz}"))
        from_left = g % 2 == 0 if dz in (0, -4, 4) else dz < 0
        if (dx < 0) == from_left:
            go(ref, g, "near" if abs(dz) < 2 else "mid" if abs(dz) < 4 else "far", -dx, 0)

    def project(k):
        origin = (ctx + k) % 4
        rows = heads[pl.ds(origin * 8, 8)].reshape(128, 2048)
        product = nt_dot(rows, proj[...]).astype(BF16)
        partial[origin] = permuted(by_target, product).reshape(8, 16, 224)
        sums[origin, tp] = partial[origin, tp]
        for dy in (2, 1, 3, 0):
            for other in (False, True):
                if dy or other:
                    device = at_tp(dy, other)
                    send(SUMS, partial.at[origin, device[1]], sums.at[origin, tp], raw_sem.at[2], device)

    def by_target(r):
        j, rest = r // 16, r % 16
        return (rest // 2) * 16 + 2 * j + rest % 2

    def opposite(name, count):
        for g in range(GROUPS):
            arrived(heads.at[pl.ds(0, count), :, columns(B, g)], sem_of(g, name))

    load_proj.wait()
    for what, *which in ORDER:
        if what == "L":
            attend(*which)
            launch(*which)
        elif what == "P":
            if which[0] == 0:
                opposite("near", 3)
                project(0)
            else:
                opposite("mid", 4)
                project(1)
                project(3)
        else:
            {"a": a_launch, "A": a_step, "b": b_step, "x": x_step}[what](*which)
    opposite("far", 1)
    project(2)
    every = sums.reshape(32, 16, 224)
    arrived(every.at[pl.ds(0, 28)], raw_sem.at[2])
    totals = []
    for origin in range(4):
        total = jnp.zeros((16, 224), F32)
        for source in range(8):
            total = total + sums[origin, source].astype(F32)
        totals.append(total.astype(BF16))

    def by_slot(r):
        return ((r // 2) % 4) * 16 + ((r // 8) % 2) * 8 + (r // 16) * 2 + r % 2

    out_ref[...] = permuted(by_slot, jnp.concatenate(totals, axis=0))
    all_sent(LIVE, live.at[pl.ds(0, 7)])
    all_sent(RAW, raw.at[pl.ds(0, 7)])
    all_sent(KEYS, value_up.reshape(8192, 128).at[pl.ds(0, 31 * 144)])
    all_sent(HEADS, heads.at[pl.ds(0, 31)])
    all_sent(SUMS, every.at[pl.ds(0, 28)])


def on_device(cache, lengths, slots, parents, nope, rope, latent_rows, key_up, value_up, proj):
    anywhere = pl.BlockSpec(memory_space=pl.ANY)
    in_vmem = pl.BlockSpec(memory_space=pltpu.VMEM)
    in_smem = pl.BlockSpec(memory_space=pltpu.SMEM)
    dma = pltpu.SemaphoreType.DMA
    out = pl.pallas_call(
        kernel,
        out_shape=jax.ShapeDtypeStruct((64, 224), BF16),
        in_specs=[anywhere, in_smem, in_smem] + [anywhere] * 7,
        out_specs=in_vmem,
        scratch_shapes=[
            pltpu.VMEM((8, 144, 128), BF16),
            pltpu.VMEM((8, 8, 128), jnp.int32),
            pltpu.VMEM((576, 1024), BF16),
            pltpu.VMEM((1, 64), jnp.int32),
            pltpu.VMEM((8, 2, 16, 128), BF16),
            pltpu.VMEM((8, 2, 16, 64), BF16),
            pltpu.VMEM((64, 576), BF16),
            pltpu.VMEM((16, 128, 512), BF16),
            pltpu.VMEM((16, 512, 128), BF16),
            pltpu.VMEM((224, 2048), BF16),
            pltpu.VMEM((256, 576), BF16),
            pltpu.VMEM((32, 16, 2048), BF16),
            pltpu.VMEM((4, 8, 16, 224), BF16),
            pltpu.VMEM((4, 8, 16, 224), BF16),
            dma((8,)), dma((3,)), dma((16,)), dma((GROUPS * len(HEAD_SEMS),)), dma((5,)),
        ],
        compiler_params=pltpu.CompilerParams(
            collective_id=0, has_side_effects=True, vmem_limit_bytes=58 * 1024 * 1024
        ),
        name="tree_attention",
    )(
        cache[0].T, lengths, slots, parents,
        nope.reshape(8, 8, 16, 128), rope.reshape(8, 8, 16, 64), latent_rows.reshape(latent_rows.shape[1:]),
        key_up, value_up, proj.T,
    )
    return out.reshape(8, 8, 224)


def solution(mesh):
    return jax.shard_map(
        on_device,
        mesh=mesh,
        in_specs=(
            P("dec", "ctx", None),
            P("dec"),
            P(),
            P("dec", None),
            P("dec", None, "tp", None),
            P("dec", None, "tp", None),
            P("dec", None, None),
            P("tp", None, None),
            P("tp", None, None),
            P("tp", ("ctx", "dec")),
        ),
        out_specs=P(None, "tp", ("ctx", "dec")),
        check_vma=False,
    )
```

```python
import math

import jax
import jax.numpy as jnp
from jax import lax
from jax.experimental import pallas as pl
from jax.experimental.pallas import tpu as pltpu
from jax.sharding import PartitionSpec as P

MESH = pl.DeviceIdType.MESH
F32 = jnp.float32
BF16 = jnp.bfloat16
GROUPS = 2
DEAD = -1e30
OFFSETS = [0, -1, 1, -2, 2, -3, 3, -4, 4]
HEAD_SEMS = ["a", "near", "mid", "far"]
HEAD_SEMS += [f"{part}{dz}" for part in ("a", "b") for dz in OFFSETS[1:]]
HEAD_SEMS += [f"x{side}{dz}" for side in "-+" for dz in OFFSETS]

ORDER = [
    ("L", 0), ("L", 1), ("b", 0, -1), ("b", 0, 1), ("x", 0, -1, 0), ("a", 0), ("x", 0, 1, 0), ("b", 1, -1),
    ("b", 1, 1), ("x", 1, 1, 0), ("a", 1), ("x", 1, -1, 0), ("b", 0, -2), ("x", 0, 1, -1), ("b", 0, 2),
    ("x", 0, -1, -1), ("x", 0, 1, 1), ("x", 0, -1, 1), ("A", 0, -1), ("A", 0, 1), ("x", 1, -1, -1), ("x", 1, 1, -1),
    ("b", 1, -2), ("b", 1, 2), ("x", 1, -1, 1), ("x", 1, 1, 1), ("x", 0, -1, -2), ("A", 1, -1), ("A", 1, 1),
    ("x", 0, 1, -2), ("x", 0, -1, 2), ("b", 0, -3), ("b", 0, 3), ("x", 0, 1, 2), ("b", 0, -4), ("x", 1, 1, -2),
    ("A", 0, 2), ("x", 1, -1, -2), ("x", 1, 1, 2), ("b", 1, 3), ("x", 1, -1, 2), ("A", 0, -2), ("b", 1, -3),
    ("x", 0, 1, -3), ("x", 0, -1, -3), ("b", 1, 4), ("x", 0, 1, 3), ("x", 0, -1, 3), ("A", 1, -2), ("x", 0, -1, -4),
    ("A", 1, 2), ("x", 0, 1, -4), ("P", 0), ("x", 1, -1, 3), ("A", 0, 3), ("x", 1, 1, 3), ("x", 1, -1, -3), ("A", 0, -3),
    ("x", 1, 1, -3), ("x", 1, 1, 4), ("x", 1, -1, 4), ("A", 0, 4), ("A", 0, -4), ("A", 1, 3), ("A", 1, -3), ("P", 1),
    ("A", 1, 4), ("A", 1, -4),
]


def nt_dot(a, b):
    return lax.dot_general(a, b, (((1,), (1,)), ((), ())), preferred_element_type=F32)


def nn_dot(a, b):
    return jnp.dot(a, b, preferred_element_type=F32)


def permuted(source_of, value):
    rows = value.shape[0]
    r = lax.broadcasted_iota(jnp.int32, (rows, rows), 0)
    s = lax.broadcasted_iota(jnp.int32, (rows, rows), 1)
    select = jnp.where(source_of(r) == s, 1.0, 0.0).astype(BF16)
    return nn_dot(select, value).astype(BF16)


def kernel(
    cache_ref, length_ref, slots_ref, parents_ref, nope_ref, rope_ref, latent_ref, key_up_ref, value_up_ref, proj_ref,
    out_ref,
    slot_ref, raw, live, keys, parents, nope, rope, tree_rows, key_up, value_up, proj, proj_t, queries, heads, partial, sums,
    local_sem, raw_sem, key_sem, head_sem, send_sem,
):
    ctx, tp, dec = lax.axis_index("ctx"), lax.axis_index("tp"), lax.axis_index("dec")
    x, z_lo = dec // 2, dec % 2
    y, core = tp // 2, tp % 2
    z = ctx * 2 + z_lo
    nodes, head_count = 16, 16
    scale = 1.0 / math.sqrt(192.0)

    def at_x(dx, dz=0):
        xx, zz = (x + dx + 4) % 4, (z + dz + 8) % 8
        return (zz // 2, tp, xx * 2 + zz % 2)

    def at_tp(dy, other_core=False):
        core_there = 1 - core if other_core else core
        return (ctx, ((y + dy) % 4) * 2 + core_there, dec)

    def at_dec(k):
        return (ctx, tp, (dec + k) % 8)

    def at_ctx(k):
        return ((ctx + k) % 4, tp, dec)

    peers = [at_dec(k) for k in range(1, 8)]
    peers += [at_ctx(k) for k in range(1, 4)]
    peers += [at_tp(dy) for dy in (1, 2, 3)] + [at_tp(dy, True) for dy in range(4)]
    away = (z + 7 + 2 * z_lo) % 8
    peers.append((away // 2, tp, x * 2 + away % 2))

    LIVE, RAW, KEYS, HEADS, SUMS = range(5)

    def described(src, dst, kind, sem, device):
        return pltpu.make_async_remote_copy(
            src_ref=src, dst_ref=dst, send_sem=send_sem.at[kind], recv_sem=sem,
            device_id=device, device_id_type=MESH,
        )

    def send(kind, ref, dst, sem, device):
        described(ref, dst, kind, sem, device).start()

    def arrived(dst, sem):
        described(dst, dst, 0, sem, at_dec(1)).wait_recv()

    def all_sent(kind, as_many_bytes):
        described(as_many_bytes, as_many_bytes, kind, raw_sem.at[0], at_dec(1)).wait_send()

    loads = []

    def load(src, dst):
        copy = pltpu.make_async_copy(src, dst, local_sem.at[len(loads)])
        copy.start()
        loads.append(copy)
        return copy

    own_rows = cache_ref.at[pl.ds(pl.multiple_of(y * 144, 16), 144), pl.ds(pl.multiple_of(core * 128, 128), 128)]
    load_slot = load(slots_ref, slot_ref)
    load_raw = load(own_rows, raw.at[dec])
    load_nope = load(nope_ref.at[:, pl.ds(ctx * 2, 2)], nope)
    load_rope = load(rope_ref.at[:, pl.ds(ctx * 2, 2)], rope)
    load_parents = load(parents_ref, parents)
    load_tree = load(latent_ref, tree_rows)
    load_key_up = load(key_up_ref, key_up)
    load_value_up = load(value_up_ref, value_up)
    load_proj = load(proj_ref, proj)

    barrier = pltpu.get_barrier_semaphore()
    for peer in peers:
        pl.semaphore_signal(barrier, inc=1, device_id=peer, device_id_type=MESH)
    live[dec] = jnp.full((8, 128), length_ref[0], jnp.int32)
    pl.semaphore_wait(barrier, len(peers))

    for k in range(1, 8):
        send(LIVE, live.at[dec], live.at[dec], raw_sem.at[1], at_dec(k))
        send(RAW, own_rows, raw.at[dec], raw_sem.at[0], at_dec(k))

    j_at = lax.broadcasted_iota(jnp.int32, (64, 64), 0)
    i_at = lax.broadcasted_iota(jnp.int32, (64, 64), 1)
    load_parents.wait()
    closure = jnp.where((parents[...] == j_at) | (i_at == j_at), 1.0, 0.0)
    for _ in range(6):
        closure = jnp.minimum(nn_dot(closure.astype(BF16), closure.astype(BF16)), 1.0)
    row = lax.broadcasted_iota(jnp.int32, (128, 64), 0) % 16
    own_node = lax.broadcasted_iota(jnp.int32, (128, 64), 1) == 8 * (row // 2) + 2 * ctx + row % 2
    on_path = nt_dot(jnp.where(own_node, 1.0, 0.0).astype(BF16), closure.astype(BF16))
    tree_bias = (on_path - 1.0) * 1e30

    def by_head(r):
        return (r % 16) * 16 + r // 16

    load_nope.wait()
    load_rope.wait()
    nope_rows = permuted(by_head, nope[...].reshape(256, 128))
    rope_rows = permuted(by_head, rope[...].reshape(256, 64))
    queries[:, 512:576] = rope_rows
    load_key_up.wait()
    for h in range(head_count):
        rows = slice(h * nodes, (h + 1) * nodes)
        queries[rows, 0:512] = nn_dot(nope_rows[rows], key_up[h]).astype(BF16)

    load_proj.wait()
    proj_t[...] = proj[...].T

    load_raw.wait()
    arrived(live.at[pl.ds(0, 7)], raw_sem.at[1])
    arrived(raw.at[pl.ds(0, 7)], raw_sem.at[0])
    load_slot.wait()
    wanted = slot_ref[dec]
    position = lax.broadcasted_iota(jnp.int32, (8, 128), 1)
    length = live[wanted]
    bias = jnp.concatenate(
        [jnp.where(position + start < length, 0.0, DEAD)[0:1] for start in range(0, 1024, 128)], axis=1
    )

    def key_part(c, t):
        rows = pl.ds(pl.multiple_of((t // 2) * 144, 16), 144)
        return keys.at[rows, pl.ds(pl.multiple_of(c * 256 + (t % 2) * 128, 128), 128)]

    key_part(ctx, tp)[...] = raw[wanted]

    def key_piece(k, t, sem, device):
        c = (ctx + k) % 4
        send(KEYS, key_part(c, t), key_part(c, t), key_sem.at[sem], device)

    def come_key(k, t, sem):
        arrived(key_part((ctx + k) % 4, t), key_sem.at[sem])

    for k in (1, 3, 2):
        key_piece(0, tp, (4 - k) * 4, at_ctx(k))
    def along_y(k):
        if k:
            come_key(k, tp, k * 4)
        for dy in (1, 3, 2):
            key_piece(k, tp, k * 4 + 4 - dy, at_tp(dy))
        key_piece(k, tp, 0, at_tp(0, True))

    def to_other_core(k):
        for dy in (1, 3, 2):
            come_key(k, at_tp(dy)[1], k * 4 + dy)
            key_piece(k, at_tp(dy)[1], 0, at_tp(0, True))

    along_y(0)
    along_y(1)
    along_y(3)
    to_other_core(0)
    along_y(2)
    for k in (1, 3, 2):
        to_other_core(k)
    arrived(keys.at[pl.ds(0, 288)], key_sem.at[0])

    load_tree.wait()
    load_value_up.wait()

    group_heads = head_count // GROUPS
    group_rows = group_heads * nodes

    def attend(g):
        q = queries[g * group_rows : (g + 1) * group_rows, :]
        s = nn_dot(q, keys[...]) * scale + bias
        s_tree = nt_dot(q, tree_rows[...]) * scale + tree_bias[:group_rows]
        peak = jnp.maximum(jnp.max(s, axis=-1, keepdims=True), jnp.max(s_tree, axis=-1, keepdims=True))
        e = jnp.exp(s - peak)
        e_tree = jnp.exp(s_tree - peak)
        total = jnp.sum(e, axis=-1, keepdims=True) + jnp.sum(e_tree, axis=-1, keepdims=True)
        o = nt_dot(e.astype(BF16), keys[0:512, :])
        o = o + nn_dot(e_tree.astype(BF16), tree_rows[:, 0:512])
        o = (o / total).astype(BF16)
        for h in range(group_heads):
            head = g * group_heads + h
            done = nn_dot(o[h * nodes : (h + 1) * nodes], value_up[head]).astype(BF16)
            heads[z * 4 + x, :, head * 128 : (head + 1) * 128] = done

    a_width = group_heads * 3 // 8 * 128
    b_width = group_heads * 128 - a_width

    A, B = 0, 1

    def columns(part, g):
        start = g * group_heads * 128 + (0 if part == A else a_width)
        return pl.ds(start, a_width if part == A else b_width)

    def block(part, g, dx, dz):
        return heads.at[((z + dz + 8) % 8) * 4 + (x + dx + 4) % 4, :, columns(part, g)]

    def column_blocks(g, dz, first, count):
        return heads.at[pl.ds(((z + dz + 8) % 8) * 4 + first, count), :, columns(A, g)]

    def sem_of(g, name):
        return head_sem.at[g * len(HEAD_SEMS) + HEAD_SEMS.index(name)]

    def go(ref, g, name, dx, dz):
        send(HEADS, ref, ref, sem_of(g, name), at_x(dx, dz))

    def far_side(part, g):
        return 1 if (g % 2 == 0) == (part == B) else -1

    def launch(g):
        own = block(B, g, 0, 0)
        go(own, g, "b-1", 0, 1)
        go(own, g, "b1", 0, -1)
        for dx in (1, -1, 2):
            go(block(A, g, 0, 0), g, "a", dx, 0)
        go(own, g, "x-0", 1, 0)
        go(own, g, "x+0", -1, 0)

    def a_launch(g):
        arrived(heads.at[pl.ds(0, 3), :, columns(A, g)], sem_of(g, "a"))
        whole = column_blocks(g, 0, 0, 4)
        go(whole, g, "a-1", 0, 1)
        go(whole, g, "a1", 0, -1)

    def b_step(g, dz):
        ref = block(B, g, 0, dz)
        arrived(ref, sem_of(g, f"b{dz}"))
        onward = 1 if dz < 0 else -1
        if abs(dz) <= 2:
            go(ref, g, f"b{dz - onward}", 0, onward)
        if abs(dz) == 2 and onward == far_side(B, g):
            go(ref, g, f"b{dz - 2 * onward}", 0, 2 * onward)
        go(ref, g, f"x-{dz}", 1, 0)
        go(ref, g, f"x+{dz}", -1, 0)

    def a_step(g, dz):
        onward = 1 if dz < 0 else -1
        half = 0 if onward == 1 else 2
        if abs(dz) == 4:
            arrived(column_blocks(g, dz, half, 2), sem_of(g, f"a{dz}"))
            return
        whole = column_blocks(g, dz, 0, 4)
        arrived(whole, sem_of(g, f"a{dz}"))
        if abs(dz) <= 2:
            go(whole, g, f"a{dz - onward}", 0, onward)
        if abs(dz) == 2:
            go(column_blocks(g, dz, half, 2), g, f"a{dz - 2 * onward}", 0, 2 * onward)

    def x_step(g, dx, dz):
        ref = block(B, g, dx, dz)
        arrived(ref, sem_of(g, f"x{'-' if dx < 0 else '+'}{dz}"))
        from_left = g % 2 == 0 if dz in (0, -4, 4) else dz < 0
        if (dx < 0) == from_left:
            go(ref, g, "near" if abs(dz) < 2 else "mid" if abs(dz) < 4 else "far", -dx, 0)

    def project(k):
        origin = (ctx + k) % 4
        rows = heads[pl.ds(origin * 8, 8)].reshape(128, 2048)
        product = nn_dot(rows, proj_t[...]).astype(BF16)
        partial[origin] = permuted(by_target, product).reshape(8, 16, 224)
        sums[origin, tp] = partial[origin, tp]
        for dy in (2, 1, 3, 0):
            for other in (False, True):
                if dy or other:
                    device = at_tp(dy, other)
                    send(SUMS, partial.at[origin, device[1]], sums.at[origin, tp], raw_sem.at[2], device)

    def by_target(r):
        j, rest = r // 16, r % 16
        return (rest // 2) * 16 + 2 * j + rest % 2

    def opposite(name, count):
        for g in range(GROUPS):
            arrived(heads.at[pl.ds(0, count), :, columns(B, g)], sem_of(g, name))

    for what, *which in ORDER:
        if what == "L":
            attend(*which)
            launch(*which)
        elif what == "P":
            if which[0] == 0:
                opposite("near", 3)
                project(0)
            else:
                opposite("mid", 4)
                project(1)
                project(3)
        else:
            {"a": a_launch, "A": a_step, "b": b_step, "x": x_step}[what](*which)
    opposite("far", 1)
    project(2)
    every = sums.reshape(32, 16, 224)
    arrived(every.at[pl.ds(0, 28)], raw_sem.at[2])
    totals = []
    for origin in range(4):
        total = jnp.zeros((16, 224), F32)
        for source in range(8):
            total = total + sums[origin, source].astype(F32)
        totals.append(total.astype(BF16))

    def by_slot(r):
        return ((r // 2) % 4) * 16 + ((r // 8) % 2) * 8 + (r // 16) * 2 + r % 2

    out_ref[...] = permuted(by_slot, jnp.concatenate(totals, axis=0))
    all_sent(LIVE, live.at[pl.ds(0, 7)])
    all_sent(RAW, raw.at[pl.ds(0, 7)])
    all_sent(KEYS, value_up.reshape(8192, 128).at[pl.ds(0, 31 * 144)])
    all_sent(HEADS, heads.at[pl.ds(0, 31)])
    all_sent(SUMS, every.at[pl.ds(0, 28)])


def on_device(cache, lengths, slots, parents, nope, rope, latent_rows, key_up, value_up, proj):
    anywhere = pl.BlockSpec(memory_space=pl.ANY)
    in_vmem = pl.BlockSpec(memory_space=pltpu.VMEM)
    dma = pltpu.SemaphoreType.DMA
    out = pl.pallas_call(
        kernel,
        out_shape=jax.ShapeDtypeStruct((64, 224), BF16),
        in_specs=[anywhere, pl.BlockSpec(memory_space=pltpu.SMEM)] + [anywhere] * 8,
        out_specs=in_vmem,
        scratch_shapes=[
            pltpu.SMEM((8,), jnp.int32),
            pltpu.VMEM((8, 144, 128), BF16),
            pltpu.VMEM((8, 8, 128), jnp.int32),
            pltpu.VMEM((576, 1024), BF16),
            pltpu.VMEM((1, 64), jnp.int32),
            pltpu.VMEM((8, 2, 16, 128), BF16),
            pltpu.VMEM((8, 2, 16, 64), BF16),
            pltpu.VMEM((64, 576), BF16),
            pltpu.VMEM((16, 128, 512), BF16),
            pltpu.VMEM((16, 512, 128), BF16),
            pltpu.VMEM((224, 2048), BF16),
            pltpu.VMEM((2048, 224), BF16),
            pltpu.VMEM((256, 576), BF16),
            pltpu.VMEM((32, 16, 2048), BF16),
            pltpu.VMEM((4, 8, 16, 224), BF16),
            pltpu.VMEM((4, 8, 16, 224), BF16),
            dma((9,)), dma((3,)), dma((16,)), dma((GROUPS * len(HEAD_SEMS),)), dma((5,)),
        ],
        compiler_params=pltpu.CompilerParams(
            collective_id=0, has_side_effects=True, vmem_limit_bytes=58 * 1024 * 1024
        ),
        name="tree_attention",
    )(
        cache[0].T, lengths, slots, parents,
        nope.reshape(8, 8, 16, 128), rope.reshape(8, 8, 16, 64), latent_rows.reshape(latent_rows.shape[1:]),
        key_up, value_up, proj.T,
    )
    return out.reshape(8, 8, 224)


def solution(mesh):
    return jax.shard_map(
        on_device,
        mesh=mesh,
        in_specs=(
            P("dec", "ctx", None),
            P("dec"),
            P(),
            P("dec", None),
            P("dec", None, "tp", None),
            P("dec", None, "tp", None),
            P("dec", None, None),
            P("tp", None, None),
            P("tp", None, None),
            P("tp", ("ctx", "dec")),
        ),
        out_specs=P(None, "tp", ("ctx", "dec")),
        check_vma=False,
    )
```

```python
import math

import jax
import jax.numpy as jnp
from jax import lax
from jax.experimental import pallas as pl
from jax.experimental.pallas import tpu as pltpu
from jax.sharding import PartitionSpec as P

MESH = pl.DeviceIdType.MESH
F32 = jnp.float32
BF16 = jnp.bfloat16
GROUPS = 2
DEAD = -1e30
OFFSETS = [0, -1, 1, -2, 2, -3, 3, -4, 4]
HEAD_SEMS = ["a", "near", "mid", "far"]
HEAD_SEMS += [f"{part}{dz}" for part in ("a", "b") for dz in OFFSETS[1:]]
HEAD_SEMS += [f"x{dz}" for dz in OFFSETS]

ORDER = [
    ("L", 0), ("L", 1), ("b", 0, -1), ("b", 0, 1), ("x", 0, 0), ("a", 0), ("b", 1, -1), ("b", 1, 1), ("x", 1, 0),
    ("a", 1), ("b", 0, -2), ("b", 0, 2), ("x", 0, -1), ("x", 0, 1), ("A", 0, -1), ("A", 0, 1), ("x", 1, -1),
    ("b", 1, -2), ("b", 1, 2), ("x", 1, 1), ("x", 0, -2), ("A", 1, -1), ("A", 1, 1), ("b", 0, -3), ("b", 0, 3),
    ("x", 0, 2), ("b", 0, -4), ("A", 0, 2), ("x", 1, -2), ("x", 1, 2), ("b", 1, 3), ("A", 0, -2), ("b", 1, -3),
    ("x", 0, -3), ("b", 1, 4), ("x", 0, 3), ("A", 1, -2), ("x", 0, -4), ("A", 1, 2), ("P", 0), ("A", 0, 3),
    ("x", 1, 3), ("x", 1, -3), ("A", 0, -3), ("x", 1, 4), ("A", 0, 4), ("A", 0, -4), ("A", 1, 3), ("A", 1, -3),
    ("P", 1), ("A", 1, 4), ("A", 1, -4),
]


def nt_dot(a, b):
    return lax.dot_general(a, b, (((1,), (1,)), ((), ())), preferred_element_type=F32)


def nn_dot(a, b):
    return jnp.dot(a, b, preferred_element_type=F32)


def permuted(source_of, value):
    rows = value.shape[0]
    r = lax.broadcasted_iota(jnp.int32, (rows, rows), 0)
    s = lax.broadcasted_iota(jnp.int32, (rows, rows), 1)
    select = jnp.where(source_of(r) == s, 1.0, 0.0).astype(BF16)
    return nn_dot(select, value).astype(BF16)


def kernel(
    cache_ref, length_ref, slots_ref, parents_ref, nope_ref, rope_ref, latent_ref, key_up_ref, value_up_ref, proj_ref,
    out_ref,
    slot_ref, raw, live, keys, parents, nope, rope, tree_rows, key_up, value_up, proj, proj_t, queries, heads, partial, sums,
    local_sem, raw_sem, key_sem, head_sem, send_sem,
):
    ctx, tp, dec = lax.axis_index("ctx"), lax.axis_index("tp"), lax.axis_index("dec")
    x, z_lo = dec // 2, dec % 2
    y, core = tp // 2, tp % 2
    z = ctx * 2 + z_lo
    nodes, head_count = 16, 16
    scale = 1.0 / math.sqrt(192.0)

    def at_x(dx, dz=0):
        xx, zz = (x + dx + 4) % 4, (z + dz + 8) % 8
        return (zz // 2, tp, xx * 2 + zz % 2)

    def at_tp(dy, other_core=False):
        core_there = 1 - core if other_core else core
        return (ctx, ((y + dy) % 4) * 2 + core_there, dec)

    def at_dec(k):
        return (ctx, tp, (dec + k) % 8)

    def at_ctx(k):
        return ((ctx + k) % 4, tp, dec)

    peers = [at_dec(k) for k in range(1, 8)]
    peers += [at_ctx(k) for k in range(1, 4)]
    peers += [at_tp(dy) for dy in (1, 2, 3)] + [at_tp(dy, True) for dy in range(4)]
    away = (z + 7 + 2 * z_lo) % 8
    peers.append((away // 2, tp, x * 2 + away % 2))

    LIVE, RAW, KEYS, HEADS, SUMS = range(5)

    def described(src, dst, kind, sem, device):
        return pltpu.make_async_remote_copy(
            src_ref=src, dst_ref=dst, send_sem=send_sem.at[kind], recv_sem=sem,
            device_id=device, device_id_type=MESH,
        )

    def send(kind, ref, dst, sem, device):
        described(ref, dst, kind, sem, device).start()

    def arrived(dst, sem):
        described(dst, dst, 0, sem, at_dec(1)).wait_recv()

    def all_sent(kind, as_many_bytes):
        described(as_many_bytes, as_many_bytes, kind, raw_sem.at[0], at_dec(1)).wait_send()

    loads = []

    def load(src, dst):
        copy = pltpu.make_async_copy(src, dst, local_sem.at[len(loads)])
        copy.start()
        loads.append(copy)
        return copy

    own_rows = cache_ref.at[pl.ds(pl.multiple_of(y * 144, 16), 144), pl.ds(pl.multiple_of(core * 128, 128), 128)]
    load_slot = load(slots_ref, slot_ref)
    load_raw = load(own_rows, raw.at[dec])
    load_nope = load(nope_ref.at[:, pl.ds(ctx * 2, 2)], nope)
    load_rope = load(rope_ref.at[:, pl.ds(ctx * 2, 2)], rope)
    load_parents = load(parents_ref, parents)
    load_tree = load(latent_ref, tree_rows)
    load_key_up = load(key_up_ref, key_up)
    load_value_up = load(value_up_ref, value_up)
    load_proj = load(proj_ref, proj)

    barrier = pltpu.get_barrier_semaphore()
    for peer in peers:
        pl.semaphore_signal(barrier, inc=1, device_id=peer, device_id_type=MESH)
    live[dec] = jnp.full((8, 128), length_ref[0], jnp.int32)
    pl.semaphore_wait(barrier, len(peers))

    load_raw.wait()
    for k in range(1, 8):
        send(RAW, raw.at[dec], raw.at[dec], raw_sem.at[0], at_dec(k))
    for k in range(1, 8):
        send(LIVE, live.at[dec], live.at[dec], raw_sem.at[1], at_dec(k))

    j_at = lax.broadcasted_iota(jnp.int32, (64, 64), 0)
    i_at = lax.broadcasted_iota(jnp.int32, (64, 64), 1)
    load_parents.wait()
    closure = jnp.where((parents[...] == j_at) | (i_at == j_at), 1.0, 0.0)
    for _ in range(6):
        closure = jnp.minimum(nn_dot(closure.astype(BF16), closure.astype(BF16)), 1.0)
    row = lax.broadcasted_iota(jnp.int32, (128, 64), 0) % 16
    own_node = lax.broadcasted_iota(jnp.int32, (128, 64), 1) == 8 * (row // 2) + 2 * ctx + row % 2
    on_path = nt_dot(jnp.where(own_node, 1.0, 0.0).astype(BF16), closure.astype(BF16))
    tree_bias = (on_path - 1.0) * 1e30

    def by_head(r):
        return (r % 16) * 16 + r // 16

    load_nope.wait()
    load_rope.wait()
    nope_rows = permuted(by_head, nope[...].reshape(256, 128))
    rope_rows = permuted(by_head, rope[...].reshape(256, 64))
    queries[:, 512:576] = rope_rows

    arrived(raw.at[pl.ds(0, 7)], raw_sem.at[0])
    load_slot.wait()
    wanted = slot_ref[dec]
    def key_part(c, t):
        rows = pl.ds(pl.multiple_of((t // 2) * 144, 16), 144)
        return keys.at[rows, pl.ds(pl.multiple_of(c * 256 + (t % 2) * 128, 128), 128)]

    key_part(ctx, tp)[...] = raw[wanted]

    def key_piece(k, t, sem, device):
        c = (ctx + k) % 4
        send(KEYS, key_part(c, t), key_part(c, t), key_sem.at[sem], device)

    def come_key(k, t, sem):
        arrived(key_part((ctx + k) % 4, t), key_sem.at[sem])

    for k in (1, 3, 2):
        key_piece(0, tp, (4 - k) * 4, at_ctx(k))
    def along_y(k):
        if k:
            come_key(k, tp, k * 4)
        for dy in (1, 3, 2):
            key_piece(k, tp, k * 4 + 4 - dy, at_tp(dy))
        key_piece(k, tp, 0, at_tp(0, True))

    def to_other_core(k):
        for dy in (1, 3, 2):
            come_key(k, at_tp(dy)[1], k * 4 + dy)
            key_piece(k, at_tp(dy)[1], 0, at_tp(0, True))

    along_y(0)
    load_key_up.wait()
    for h in range(head_count):
        rows = slice(h * nodes, (h + 1) * nodes)
        queries[rows, 0:512] = nn_dot(nope_rows[rows], key_up[h]).astype(BF16)
    along_y(1)
    along_y(3)
    to_other_core(0)
    along_y(2)
    load_proj.wait()
    proj_t[...] = proj[...].T
    arrived(live.at[pl.ds(0, 7)], raw_sem.at[1])
    position = lax.broadcasted_iota(jnp.int32, (8, 128), 1)
    length = live[wanted]
    bias = jnp.concatenate(
        [jnp.where(position + start < length, 0.0, DEAD)[0:1] for start in range(0, 1024, 128)], axis=1
    )
    for k in (1, 3, 2):
        to_other_core(k)
    arrived(keys.at[pl.ds(0, 288)], key_sem.at[0])

    load_tree.wait()
    load_value_up.wait()

    group_heads = head_count // GROUPS
    group_rows = group_heads * nodes

    def attend(g):
        q = queries[g * group_rows : (g + 1) * group_rows, :]
        s = nn_dot(q, keys[...]) * scale + bias
        s_tree = nt_dot(q, tree_rows[...]) * scale + tree_bias[:group_rows]
        peak = jnp.maximum(jnp.max(s, axis=-1, keepdims=True), jnp.max(s_tree, axis=-1, keepdims=True))
        e = jnp.exp(s - peak)
        e_tree = jnp.exp(s_tree - peak)
        total = jnp.sum(e, axis=-1, keepdims=True) + jnp.sum(e_tree, axis=-1, keepdims=True)
        o = nt_dot(e.astype(BF16), keys[0:512, :])
        o = o + nn_dot(e_tree.astype(BF16), tree_rows[:, 0:512])
        o = (o / total).astype(BF16)
        for h in range(group_heads):
            head = g * group_heads + h
            done = nn_dot(o[h * nodes : (h + 1) * nodes], value_up[head]).astype(BF16)
            heads[z * 4 + x, :, head * 128 : (head + 1) * 128] = done

    a_width = group_heads * 3 // 8 * 128
    b_width = group_heads * 128 - a_width

    A, B = 0, 1

    def columns(part, g):
        start = g * group_heads * 128 + (0 if part == A else a_width)
        return pl.ds(start, a_width if part == A else b_width)

    def block(part, g, dx, dz):
        return heads.at[((z + dz + 8) % 8) * 4 + (x + dx + 4) % 4, :, columns(part, g)]

    def column_blocks(g, dz, first, count):
        return heads.at[pl.ds(((z + dz + 8) % 8) * 4 + first, count), :, columns(A, g)]

    def sem_of(g, name):
        return head_sem.at[g * len(HEAD_SEMS) + HEAD_SEMS.index(name)]

    def go(ref, g, name, dx, dz):
        send(HEADS, ref, ref, sem_of(g, name), at_x(dx, dz))

    def far_side(part, g):
        return 1 if (g % 2 == 0) == (part == B) else -1

    def from_left(g, dz):
        return g % 2 == 0 if dz in (0, -4, 4) else dz < 0

    def distance(dz):
        return "near" if abs(dz) < 2 else "mid" if abs(dz) < 4 else "far"

    def to_x(g, dz):
        ref = block(B, g, 0, dz)
        go(ref, g, f"x{dz}" if from_left(g, dz) else distance(dz), 1, 0)
        go(ref, g, distance(dz) if from_left(g, dz) else f"x{dz}", -1, 0)

    def launch(g):
        own = block(B, g, 0, 0)
        go(own, g, "b-1", 0, 1)
        go(own, g, "b1", 0, -1)
        for dx in (1, -1, 2):
            go(block(A, g, 0, 0), g, "a", dx, 0)
        to_x(g, 0)

    def a_launch(g):
        arrived(heads.at[pl.ds(0, 3), :, columns(A, g)], sem_of(g, "a"))
        whole = column_blocks(g, 0, 0, 4)
        go(whole, g, "a-1", 0, 1)
        go(whole, g, "a1", 0, -1)

    def b_step(g, dz):
        ref = block(B, g, 0, dz)
        arrived(ref, sem_of(g, f"b{dz}"))
        onward = 1 if dz < 0 else -1
        if abs(dz) <= 2:
            go(ref, g, f"b{dz - onward}", 0, onward)
        if abs(dz) == 2 and onward == far_side(B, g):
            go(ref, g, f"b{dz - 2 * onward}", 0, 2 * onward)
        to_x(g, dz)

    def a_step(g, dz):
        onward = 1 if dz < 0 else -1
        half = 0 if onward == 1 else 2
        if abs(dz) == 4:
            arrived(column_blocks(g, dz, half, 2), sem_of(g, f"a{dz}"))
            return
        whole = column_blocks(g, dz, 0, 4)
        arrived(whole, sem_of(g, f"a{dz}"))
        if abs(dz) <= 2:
            go(whole, g, f"a{dz - onward}", 0, onward)
        if abs(dz) == 2:
            go(column_blocks(g, dz, half, 2), g, f"a{dz - 2 * onward}", 0, 2 * onward)

    def x_step(g, dz):
        dx = -1 if from_left(g, dz) else 1
        ref = block(B, g, dx, dz)
        arrived(ref, sem_of(g, f"x{dz}"))
        go(ref, g, distance(dz), -dx, 0)

    def project(k):
        origin = (ctx + k) % 4
        rows = heads[pl.ds(origin * 8, 8)].reshape(128, 2048)
        product = nn_dot(rows, proj_t[...]).astype(BF16)
        partial[origin] = permuted(by_target, product).reshape(8, 16, 224)
        sums[origin, tp] = partial[origin, tp]
        for dy in (2, 1, 3, 0):
            for other in (False, True):
                if dy or other:
                    device = at_tp(dy, other)
                    send(SUMS, partial.at[origin, device[1]], sums.at[origin, tp], raw_sem.at[2], device)

    def by_target(r):
        j, rest = r // 16, r % 16
        return (rest // 2) * 16 + 2 * j + rest % 2

    def opposite(name, count):
        for g in range(GROUPS):
            arrived(heads.at[pl.ds(0, count), :, columns(B, g)], sem_of(g, name))

    for what, *which in ORDER:
        if what == "L":
            attend(*which)
            launch(*which)
        elif what == "P":
            if which[0] == 0:
                opposite("near", 6)
                project(0)
            else:
                opposite("mid", 8)
                project(1)
                project(3)
        else:
            {"a": a_launch, "A": a_step, "b": b_step, "x": x_step}[what](*which)
    opposite("far", 2)
    project(2)
    every = sums.reshape(32, 16, 224)
    arrived(every.at[pl.ds(0, 28)], raw_sem.at[2])
    totals = []
    for origin in range(4):
        total = jnp.zeros((16, 224), F32)
        for source in range(8):
            total = total + sums[origin, source].astype(F32)
        totals.append(total.astype(BF16))

    def by_slot(r):
        return ((r // 2) % 4) * 16 + ((r // 8) % 2) * 8 + (r // 16) * 2 + r % 2

    out_ref[...] = permuted(by_slot, jnp.concatenate(totals, axis=0))
    all_sent(LIVE, live.at[pl.ds(0, 7)])
    all_sent(RAW, raw.at[pl.ds(0, 7)])
    all_sent(KEYS, value_up.reshape(8192, 128).at[pl.ds(0, 31 * 144)])
    all_sent(HEADS, heads.at[pl.ds(0, 31)])
    all_sent(SUMS, every.at[pl.ds(0, 28)])


def on_device(cache, lengths, slots, parents, nope, rope, latent_rows, key_up, value_up, proj):
    anywhere = pl.BlockSpec(memory_space=pl.ANY)
    in_vmem = pl.BlockSpec(memory_space=pltpu.VMEM)
    dma = pltpu.SemaphoreType.DMA
    out = pl.pallas_call(
        kernel,
        out_shape=jax.ShapeDtypeStruct((64, 224), BF16),
        in_specs=[anywhere, pl.BlockSpec(memory_space=pltpu.SMEM)] + [anywhere] * 8,
        out_specs=in_vmem,
        scratch_shapes=[
            pltpu.SMEM((8,), jnp.int32),
            pltpu.VMEM((8, 144, 128), BF16),
            pltpu.VMEM((8, 8, 128), jnp.int32),
            pltpu.VMEM((576, 1024), BF16),
            pltpu.VMEM((1, 64), jnp.int32),
            pltpu.VMEM((8, 2, 16, 128), BF16),
            pltpu.VMEM((8, 2, 16, 64), BF16),
            pltpu.VMEM((64, 576), BF16),
            pltpu.VMEM((16, 128, 512), BF16),
            pltpu.VMEM((16, 512, 128), BF16),
            pltpu.VMEM((224, 2048), BF16),
            pltpu.VMEM((2048, 224), BF16),
            pltpu.VMEM((256, 576), BF16),
            pltpu.VMEM((32, 16, 2048), BF16),
            pltpu.VMEM((4, 8, 16, 224), BF16),
            pltpu.VMEM((4, 8, 16, 224), BF16),
            dma((9,)), dma((3,)), dma((16,)), dma((GROUPS * len(HEAD_SEMS),)), dma((5,)),
        ],
        compiler_params=pltpu.CompilerParams(
            collective_id=0, has_side_effects=True, vmem_limit_bytes=58 * 1024 * 1024
        ),
        name="tree_attention",
    )(
        cache[0].T, lengths, slots, parents,
        nope.reshape(8, 8, 16, 128), rope.reshape(8, 8, 16, 64), latent_rows.reshape(latent_rows.shape[1:]),
        key_up, value_up, proj.T,
    )
    return out.reshape(8, 8, 224)


def solution(mesh):
    return jax.shard_map(
        on_device,
        mesh=mesh,
        in_specs=(
            P("dec", "ctx", None),
            P("dec"),
            P(),
            P("dec", None),
            P("dec", None, "tp", None),
            P("dec", None, "tp", None),
            P("dec", None, None),
            P("tp", None, None),
            P("tp", None, None),
            P("tp", ("ctx", "dec")),
        ),
        out_specs=P(None, "tp", ("ctx", "dec")),
        check_vma=False,
    )
```

```python
import math

import jax
import jax.numpy as jnp
from jax import lax
from jax.experimental import pallas as pl
from jax.experimental.pallas import tpu as pltpu
from jax.sharding import PartitionSpec as P

MESH = pl.DeviceIdType.MESH
F32 = jnp.float32
BF16 = jnp.bfloat16
GROUP_HEADS = (8, 8)
A_HEADS = (3, 3)
GROUPS = len(GROUP_HEADS)
DEAD = -1e30
OFFSETS = [0, -1, 1, -2, 2, -3, 3, -4, 4]
HEAD_SEMS = ["a", "near", "mid", "far"]
HEAD_SEMS += [f"{part}{dz}" for part in ("a", "b") for dz in OFFSETS[1:]]
HEAD_SEMS += [f"x{dz}" for dz in OFFSETS]

ORDER = [
    ("L", 0), ("L", 1), ("b", 0, -1), ("b", 0, 1), ("a", 0), ("x", 0, 0), ("b", 0, -2), ("b", 0, 2), ("b", 1, -1),
    ("b", 1, 1), ("a", 1), ("x", 1, 0), ("x", 0, -1), ("b", 1, -2), ("b", 1, 2), ("x", 0, 1), ("A", 0, -1),
    ("A", 0, 1), ("x", 0, -2), ("b", 0, -3), ("b", 0, 3), ("x", 0, 2), ("x", 1, -1), ("x", 1, 1), ("b", 0, -4),
    ("A", 1, 1), ("b", 1, 3), ("A", 1, -1), ("x", 1, -2), ("x", 1, 2), ("b", 1, -3), ("b", 1, 4), ("A", 0, -2),
    ("x", 0, -3), ("A", 0, 2), ("x", 0, 3), ("P", 0), ("A", 1, 2), ("x", 0, -4), ("A", 1, -2), ("x", 1, 3),
    ("x", 1, -3), ("A", 0, -3), ("x", 1, 4), ("A", 0, 3), ("A", 0, -4), ("A", 0, 4), ("A", 1, -3), ("A", 1, 3),
    ("P", 1), ("A", 1, -4), ("A", 1, 4),
]


def nt_dot(a, b):
    return lax.dot_general(a, b, (((1,), (1,)), ((), ())), preferred_element_type=F32)


def nn_dot(a, b):
    return jnp.dot(a, b, preferred_element_type=F32)


def permuted(source_of, value):
    rows = value.shape[0]
    r = lax.broadcasted_iota(jnp.int32, (rows, rows), 0)
    s = lax.broadcasted_iota(jnp.int32, (rows, rows), 1)
    select = jnp.where(source_of(r) == s, 1.0, 0.0).astype(BF16)
    return nn_dot(select, value).astype(BF16)


def kernel(
    cache_ref, length_ref, slots_ref, parents_ref, nope_ref, rope_ref, latent_ref, key_up_ref, value_up_ref, proj_ref,
    out_ref,
    slot_ref, raw, live, keys, parents, nope, rope, tree_rows, key_up, value_up, proj, proj_t, queries, heads, partial, sums,
    local_sem, raw_sem, key_sem, head_sem, send_sem,
):
    ctx, tp, dec = lax.axis_index("ctx"), lax.axis_index("tp"), lax.axis_index("dec")
    x, z_lo = dec // 2, dec % 2
    y, core = tp // 2, tp % 2
    z = ctx * 2 + z_lo
    nodes, head_count = 16, 16
    scale = 1.0 / math.sqrt(192.0)

    def at_x(dx, dz=0):
        xx, zz = (x + dx + 4) % 4, (z + dz + 8) % 8
        return (zz // 2, tp, xx * 2 + zz % 2)

    def at_tp(dy, other_core=False):
        core_there = 1 - core if other_core else core
        return (ctx, ((y + dy) % 4) * 2 + core_there, dec)

    def at_dec(k):
        return (ctx, tp, (dec + k) % 8)

    def at_ctx(k):
        return ((ctx + k) % 4, tp, dec)

    peers = [at_dec(k) for k in range(1, 8)]
    peers += [at_ctx(k) for k in range(1, 4)]
    peers += [at_tp(dy) for dy in (1, 2, 3)] + [at_tp(dy, True) for dy in range(4)]
    away = (z + 7 + 2 * z_lo) % 8
    peers.append((away // 2, tp, x * 2 + away % 2))

    LIVE, RAW, KEYS, HEADS, SUMS = range(5)

    def described(src, dst, kind, sem, device):
        return pltpu.make_async_remote_copy(
            src_ref=src, dst_ref=dst, send_sem=send_sem.at[kind], recv_sem=sem,
            device_id=device, device_id_type=MESH,
        )

    def send(kind, ref, dst, sem, device):
        described(ref, dst, kind, sem, device).start()

    def arrived(dst, sem):
        described(dst, dst, 0, sem, at_dec(1)).wait_recv()

    def all_sent(kind, as_many_bytes):
        described(as_many_bytes, as_many_bytes, kind, raw_sem.at[0], at_dec(1)).wait_send()

    loads = []

    def load(src, dst):
        copy = pltpu.make_async_copy(src, dst, local_sem.at[len(loads)])
        copy.start()
        loads.append(copy)
        return copy

    own_rows = cache_ref.at[pl.ds(pl.multiple_of(y * 144, 16), 144), pl.ds(pl.multiple_of(core * 128, 128), 128)]
    load_slot = load(slots_ref, slot_ref)
    load_raw = load(own_rows, raw.at[dec])
    load_nope = load(nope_ref.at[:, pl.ds(ctx * 2, 2)], nope)
    load_rope = load(rope_ref.at[:, pl.ds(ctx * 2, 2)], rope)
    load_parents = load(parents_ref, parents)
    load_tree = load(latent_ref, tree_rows)
    load_key_up = load(key_up_ref, key_up)
    load_value_up = load(value_up_ref, value_up)
    load_proj = load(proj_ref, proj)

    barrier = pltpu.get_barrier_semaphore()
    for peer in peers:
        pl.semaphore_signal(barrier, inc=1, device_id=peer, device_id_type=MESH)
    live[dec] = jnp.full((8, 128), length_ref[0], jnp.int32)
    pl.semaphore_wait(barrier, len(peers))

    load_raw.wait()
    for k in range(1, 8):
        send(RAW, raw.at[dec], raw.at[dec], raw_sem.at[0], at_dec(k))
    for k in range(1, 8):
        send(LIVE, live.at[dec], live.at[dec], raw_sem.at[1], at_dec(k))

    j_at = lax.broadcasted_iota(jnp.int32, (64, 64), 0)
    i_at = lax.broadcasted_iota(jnp.int32, (64, 64), 1)
    load_parents.wait()
    closure = jnp.where((parents[...] == j_at) | (i_at == j_at), 1.0, 0.0)
    for _ in range(6):
        closure = jnp.minimum(nn_dot(closure.astype(BF16), closure.astype(BF16)), 1.0)
    row = lax.broadcasted_iota(jnp.int32, (128, 64), 0) % 16
    own_node = lax.broadcasted_iota(jnp.int32, (128, 64), 1) == 8 * (row // 2) + 2 * ctx + row % 2
    on_path = nt_dot(jnp.where(own_node, 1.0, 0.0).astype(BF16), closure.astype(BF16))
    tree_bias = (on_path - 1.0) * 1e30

    def by_head(r):
        return (r % 16) * 16 + r // 16

    load_nope.wait()
    load_rope.wait()
    nope_rows = permuted(by_head, nope[...].reshape(256, 128))
    rope_rows = permuted(by_head, rope[...].reshape(256, 64))
    queries[:, 512:576] = rope_rows

    arrived(raw.at[pl.ds(0, 7)], raw_sem.at[0])
    load_slot.wait()
    wanted = slot_ref[dec]
    def key_part(c, t):
        rows = pl.ds(pl.multiple_of((t // 2) * 144, 16), 144)
        return keys.at[rows, pl.ds(pl.multiple_of(c * 256 + (t % 2) * 128, 128), 128)]

    key_part(ctx, tp)[...] = raw[wanted]

    def key_piece(k, t, sem, device):
        c = (ctx + k) % 4
        send(KEYS, key_part(c, t), key_part(c, t), key_sem.at[sem], device)

    def come_key(k, t, sem):
        arrived(key_part((ctx + k) % 4, t), key_sem.at[sem])

    for k in (1, 3, 2):
        key_piece(0, tp, (4 - k) * 4, at_ctx(k))
    def along_y(k):
        if k:
            come_key(k, tp, k * 4)
        for dy in (1, 3, 2):
            key_piece(k, tp, k * 4 + 4 - dy, at_tp(dy))
        key_piece(k, tp, 0, at_tp(0, True))

    def to_other_core(k):
        for dy in (1, 3, 2):
            come_key(k, at_tp(dy)[1], k * 4 + dy)
            key_piece(k, at_tp(dy)[1], 0, at_tp(0, True))

    along_y(0)
    load_key_up.wait()
    for h in range(head_count):
        rows = slice(h * nodes, (h + 1) * nodes)
        queries[rows, 0:512] = nn_dot(nope_rows[rows], key_up[h]).astype(BF16)
    along_y(1)
    along_y(3)
    to_other_core(0)
    along_y(2)
    load_proj.wait()
    proj_t[...] = proj[...].T
    arrived(live.at[pl.ds(0, 7)], raw_sem.at[1])
    position = lax.broadcasted_iota(jnp.int32, (8, 128), 1)
    length = live[wanted]
    bias = jnp.concatenate(
        [jnp.where(position + start < length, 0.0, DEAD)[0:1] for start in range(0, 1024, 128)], axis=1
    )
    for k in (1, 3, 2):
        to_other_core(k)
    arrived(keys.at[pl.ds(0, 288)], key_sem.at[0])

    load_tree.wait()
    load_value_up.wait()

    first_head = [sum(GROUP_HEADS[:g]) for g in range(GROUPS)]

    def attend(g):
        group_heads = GROUP_HEADS[g]
        group_rows = group_heads * nodes
        q = queries[first_head[g] * nodes : first_head[g] * nodes + group_rows, :]
        s = nn_dot(q, keys[...]) * scale + bias
        s_tree = nt_dot(q, tree_rows[...]) * scale + tree_bias[:group_rows]
        peak = jnp.maximum(jnp.max(s, axis=-1, keepdims=True), jnp.max(s_tree, axis=-1, keepdims=True))
        e = jnp.exp(s - peak)
        e_tree = jnp.exp(s_tree - peak)
        total = jnp.sum(e, axis=-1, keepdims=True) + jnp.sum(e_tree, axis=-1, keepdims=True)
        o = nt_dot(e.astype(BF16), keys[0:512, :])
        o = o + nn_dot(e_tree.astype(BF16), tree_rows[:, 0:512])
        o = (o / total).astype(BF16)
        for h in range(group_heads):
            head = first_head[g] + h
            done = nn_dot(o[h * nodes : (h + 1) * nodes], value_up[head]).astype(BF16)
            heads[z * 4 + x, :, head * 128 : (head + 1) * 128] = done


    A, B = 0, 1

    def columns(part, g):
        start = first_head[g] + (0 if part == A else A_HEADS[g])
        count = A_HEADS[g] if part == A else GROUP_HEADS[g] - A_HEADS[g]
        return pl.ds(start * 128, count * 128)

    def block(part, g, dx, dz):
        return heads.at[((z + dz + 8) % 8) * 4 + (x + dx + 4) % 4, :, columns(part, g)]

    def column_blocks(g, dz, first, count):
        return heads.at[pl.ds(((z + dz + 8) % 8) * 4 + first, count), :, columns(A, g)]

    def sem_of(g, name):
        return head_sem.at[g * len(HEAD_SEMS) + HEAD_SEMS.index(name)]

    def go(ref, g, name, dx, dz):
        send(HEADS, ref, ref, sem_of(g, name), at_x(dx, dz))

    def far_side(part, g):
        return 1 if (g % 2 == 0) == (part == B) else -1

    def from_left(g, dz):
        return g % 2 == 0 if dz in (0, -4, 4) else dz < 0

    def distance(dz):
        return "near" if abs(dz) < 2 else "mid" if abs(dz) < 4 else "far"

    def to_x(g, dz):
        ref = block(B, g, 0, dz)
        go(ref, g, f"x{dz}" if from_left(g, dz) else distance(dz), 1, 0)
        go(ref, g, distance(dz) if from_left(g, dz) else f"x{dz}", -1, 0)

    def launch(g):
        own = block(B, g, 0, 0)
        go(own, g, "b-1", 0, 1)
        go(own, g, "b1", 0, -1)
        go(own, g, "b-2", 0, 2)
        go(own, g, "b2", 0, -2)
        for dx in (1, -1, 2):
            go(block(A, g, 0, 0), g, "a", dx, 0)
        to_x(g, 0)

    def a_launch(g):
        arrived(heads.at[pl.ds(0, 3), :, columns(A, g)], sem_of(g, "a"))
        whole = column_blocks(g, 0, 0, 4)
        go(whole, g, "a-1", 0, 1)
        go(whole, g, "a1", 0, -1)

    def b_step(g, dz):
        ref = block(B, g, 0, dz)
        arrived(ref, sem_of(g, f"b{dz}"))
        onward = 1 if dz < 0 else -1
        if abs(dz) == 2:
            go(ref, g, f"b{dz - onward}", 0, onward)
        if abs(dz) == 2 and onward == far_side(B, g):
            go(ref, g, f"b{dz - 2 * onward}", 0, 2 * onward)
        to_x(g, dz)

    def a_step(g, dz):
        onward = 1 if dz < 0 else -1
        half = 0 if onward == 1 else 2
        if abs(dz) == 4:
            arrived(column_blocks(g, dz, half, 2), sem_of(g, f"a{dz}"))
            return
        whole = column_blocks(g, dz, 0, 4)
        arrived(whole, sem_of(g, f"a{dz}"))
        if abs(dz) <= 2:
            go(whole, g, f"a{dz - onward}", 0, onward)
        if abs(dz) == 2:
            go(column_blocks(g, dz, half, 2), g, f"a{dz - 2 * onward}", 0, 2 * onward)

    def x_step(g, dz):
        dx = -1 if from_left(g, dz) else 1
        ref = block(B, g, dx, dz)
        arrived(ref, sem_of(g, f"x{dz}"))
        go(ref, g, distance(dz), -dx, 0)

    def project(k):
        origin = (ctx + k) % 4
        rows = heads[pl.ds(origin * 8, 8)].reshape(128, 2048)
        product = nn_dot(rows, proj_t[...]).astype(BF16)
        partial[origin] = permuted(by_target, product).reshape(8, 16, 224)
        sums[origin, tp] = partial[origin, tp]
        for dy in (2, 1, 3, 0):
            for other in (False, True):
                if dy or other:
                    device = at_tp(dy, other)
                    send(SUMS, partial.at[origin, device[1]], sums.at[origin, tp], raw_sem.at[2], device)

    def by_target(r):
        j, rest = r // 16, r % 16
        return (rest // 2) * 16 + 2 * j + rest % 2

    def opposite(name, count):
        for g in range(GROUPS):
            arrived(heads.at[pl.ds(0, count), :, columns(B, g)], sem_of(g, name))

    for what, *which in ORDER:
        if what == "L":
            attend(*which)
            launch(*which)
        elif what == "P":
            if which[0] == 0:
                opposite("near", 6)
                project(0)
            else:
                opposite("mid", 8)
                project(1)
                project(3)
        else:
            {"a": a_launch, "A": a_step, "b": b_step, "x": x_step}[what](*which)
    opposite("far", 2)
    project(2)
    every = sums.reshape(32, 16, 224)
    arrived(every.at[pl.ds(0, 28)], raw_sem.at[2])
    totals = []
    for origin in range(4):
        total = jnp.zeros((16, 224), F32)
        for source in range(8):
            total = total + sums[origin, source].astype(F32)
        totals.append(total.astype(BF16))

    def by_slot(r):
        return ((r // 2) % 4) * 16 + ((r // 8) % 2) * 8 + (r // 16) * 2 + r % 2

    out_ref[...] = permuted(by_slot, jnp.concatenate(totals, axis=0))
    all_sent(LIVE, live.at[pl.ds(0, 7)])
    all_sent(RAW, raw.at[pl.ds(0, 7)])
    all_sent(KEYS, value_up.reshape(8192, 128).at[pl.ds(0, 31 * 144)])
    all_sent(HEADS, heads.at[pl.ds(0, 31)])
    all_sent(SUMS, every.at[pl.ds(0, 28)])


def on_device(cache, lengths, slots, parents, nope, rope, latent_rows, key_up, value_up, proj):
    anywhere = pl.BlockSpec(memory_space=pl.ANY)
    in_vmem = pl.BlockSpec(memory_space=pltpu.VMEM)
    dma = pltpu.SemaphoreType.DMA
    out = pl.pallas_call(
        kernel,
        out_shape=jax.ShapeDtypeStruct((64, 224), BF16),
        in_specs=[anywhere, pl.BlockSpec(memory_space=pltpu.SMEM)] + [anywhere] * 8,
        out_specs=in_vmem,
        scratch_shapes=[
            pltpu.SMEM((8,), jnp.int32),
            pltpu.VMEM((8, 144, 128), BF16),
            pltpu.VMEM((8, 8, 128), jnp.int32),
            pltpu.VMEM((576, 1024), BF16),
            pltpu.VMEM((1, 64), jnp.int32),
            pltpu.VMEM((8, 2, 16, 128), BF16),
            pltpu.VMEM((8, 2, 16, 64), BF16),
            pltpu.VMEM((64, 576), BF16),
            pltpu.VMEM((16, 128, 512), BF16),
            pltpu.VMEM((16, 512, 128), BF16),
            pltpu.VMEM((224, 2048), BF16),
            pltpu.VMEM((2048, 224), BF16),
            pltpu.VMEM((256, 576), BF16),
            pltpu.VMEM((32, 16, 2048), BF16),
            pltpu.VMEM((4, 8, 16, 224), BF16),
            pltpu.VMEM((4, 8, 16, 224), BF16),
            dma((9,)), dma((3,)), dma((16,)), dma((GROUPS * len(HEAD_SEMS),)), dma((5,)),
        ],
        compiler_params=pltpu.CompilerParams(
            collective_id=0, has_side_effects=True, vmem_limit_bytes=58 * 1024 * 1024
        ),
        name="tree_attention",
    )(
        cache[0].T, lengths, slots, parents,
        nope.reshape(8, 8, 16, 128), rope.reshape(8, 8, 16, 64), latent_rows.reshape(latent_rows.shape[1:]),
        key_up, value_up, proj.T,
    )
    return out.reshape(8, 8, 224)


def solution(mesh):
    return jax.shard_map(
        on_device,
        mesh=mesh,
        in_specs=(
            P("dec", "ctx", None),
            P("dec"),
            P(),
            P("dec", None),
            P("dec", None, "tp", None),
            P("dec", None, "tp", None),
            P("dec", None, None),
            P("tp", None, None),
            P("tp", None, None),
            P("tp", ("ctx", "dec")),
        ),
        out_specs=P(None, "tp", ("ctx", "dec")),
        check_vma=False,
    )
```

```python
import math

import jax
import jax.numpy as jnp
from jax import lax
from jax.experimental import pallas as pl
from jax.experimental.pallas import tpu as pltpu
from jax.sharding import PartitionSpec as P

MESH = pl.DeviceIdType.MESH
F32 = jnp.float32
BF16 = jnp.bfloat16
GROUP_HEADS = (8, 8)
A_HEADS = (3, 3)
GROUPS = len(GROUP_HEADS)
DEAD = -1e30
OFFSETS = [0, -1, 1, -2, 2, -3, 3, -4, 4]
HEAD_SEMS = ["a", "near", "mid", "far"]
HEAD_SEMS += [f"{part}{dz}" for part in ("a", "b") for dz in OFFSETS[1:]]
HEAD_SEMS += [f"x{dz}" for dz in OFFSETS]

ORDER = [
    ("L", 0), ("L", 1), ("b", 0, -1), ("b", 0, 1), ("a", 0), ("x", 0, 0), ("b", 0, -2), ("b", 0, 2), ("b", 1, -1),
    ("b", 1, 1), ("a", 1), ("x", 1, 0), ("x", 0, -1), ("b", 1, -2), ("b", 1, 2), ("x", 0, 1), ("A", 0, -1),
    ("A", 0, 1), ("x", 0, -2), ("b", 0, -3), ("b", 0, 3), ("x", 0, 2), ("x", 1, -1), ("x", 1, 1), ("b", 0, -4),
    ("A", 1, 1), ("b", 1, 3), ("A", 1, -1), ("x", 1, -2), ("x", 1, 2), ("b", 1, -3), ("b", 1, 4), ("A", 0, -2),
    ("x", 0, -3), ("A", 0, 2), ("x", 0, 3), ("A", 1, 2), ("x", 0, -4), ("A", 1, -2), ("x", 1, 3), ("x", 1, -3),
    ("P", 0), ("A", 0, -3), ("x", 1, 4), ("A", 0, 3), ("A", 0, -4), ("A", 0, 4), ("A", 1, -3), ("A", 1, 3), ("P", 1),
    ("A", 1, -4), ("A", 1, 4),
]


def nt_dot(a, b):
    return lax.dot_general(a, b, (((1,), (1,)), ((), ())), preferred_element_type=F32)


def nn_dot(a, b):
    return jnp.dot(a, b, preferred_element_type=F32)


def permuted(source_of, value):
    rows = value.shape[0]
    r = lax.broadcasted_iota(jnp.int32, (rows, rows), 0)
    s = lax.broadcasted_iota(jnp.int32, (rows, rows), 1)
    select = jnp.where(source_of(r) == s, 1.0, 0.0).astype(BF16)
    return nn_dot(select, value).astype(BF16)


def kernel(
    cache_ref, length_ref, slots_ref, parents_ref, nope_ref, rope_ref, latent_ref, key_up_ref, value_up_ref, proj_ref,
    out_ref,
    slot_ref, raw, live, keys, parents, nope, rope, tree_rows, key_up, value_up, proj, proj_t, queries, heads, partial, sums, totals,
    local_sem, raw_sem, key_sem, head_sem, send_sem,
):
    ctx, tp, dec = lax.axis_index("ctx"), lax.axis_index("tp"), lax.axis_index("dec")
    x, z_lo = dec // 2, dec % 2
    y, core = tp // 2, tp % 2
    z = ctx * 2 + z_lo
    nodes, head_count = 16, 16
    scale = 1.0 / math.sqrt(192.0)

    def at_x(dx, dz=0):
        xx, zz = (x + dx + 4) % 4, (z + dz + 8) % 8
        return (zz // 2, tp, xx * 2 + zz % 2)

    def at_tp(dy, other_core=False):
        core_there = 1 - core if other_core else core
        return (ctx, ((y + dy) % 4) * 2 + core_there, dec)

    def at_dec(k):
        return (ctx, tp, (dec + k) % 8)

    def at_ctx(k):
        return ((ctx + k) % 4, tp, dec)

    peers = [at_dec(k) for k in range(1, 8)]
    peers += [at_ctx(k) for k in range(1, 4)]
    peers += [at_tp(dy) for dy in (1, 2, 3)] + [at_tp(dy, True) for dy in range(4)]
    away = (z + 7 + 2 * z_lo) % 8
    peers.append((away // 2, tp, x * 2 + away % 2))

    LIVE, RAW, KEYS, HEADS, SUMS = range(5)

    def described(src, dst, kind, sem, device):
        return pltpu.make_async_remote_copy(
            src_ref=src, dst_ref=dst, send_sem=send_sem.at[kind], recv_sem=sem,
            device_id=device, device_id_type=MESH,
        )

    def send(kind, ref, dst, sem, device):
        described(ref, dst, kind, sem, device).start()

    def arrived(dst, sem):
        described(dst, dst, 0, sem, at_dec(1)).wait_recv()

    def all_sent(kind, as_many_bytes):
        described(as_many_bytes, as_many_bytes, kind, raw_sem.at[0], at_dec(1)).wait_send()

    loads = []

    def load(src, dst):
        copy = pltpu.make_async_copy(src, dst, local_sem.at[len(loads)])
        copy.start()
        loads.append(copy)
        return copy

    own_rows = cache_ref.at[pl.ds(pl.multiple_of(y * 144, 16), 144), pl.ds(pl.multiple_of(core * 128, 128), 128)]
    load_slot = load(slots_ref, slot_ref)
    load_raw = load(own_rows, raw.at[dec])
    load_nope = load(nope_ref.at[:, pl.ds(ctx * 2, 2)], nope)
    load_rope = load(rope_ref.at[:, pl.ds(ctx * 2, 2)], rope)
    load_parents = load(parents_ref, parents)
    load_tree = load(latent_ref, tree_rows)
    load_key_up = load(key_up_ref, key_up)
    load_value_up = load(value_up_ref, value_up)
    load_proj = load(proj_ref, proj)

    barrier = pltpu.get_barrier_semaphore()
    for peer in peers:
        pl.semaphore_signal(barrier, inc=1, device_id=peer, device_id_type=MESH)
    live[dec] = jnp.full((8, 128), length_ref[0], jnp.int32)
    pl.semaphore_wait(barrier, len(peers))

    load_raw.wait()
    for k in range(1, 8):
        send(RAW, raw.at[dec], raw.at[dec], raw_sem.at[0], at_dec(k))
    for k in range(1, 8):
        send(LIVE, live.at[dec], live.at[dec], raw_sem.at[1], at_dec(k))

    j_at = lax.broadcasted_iota(jnp.int32, (64, 64), 0)
    i_at = lax.broadcasted_iota(jnp.int32, (64, 64), 1)
    load_parents.wait()
    closure = jnp.where((parents[...] == j_at) | (i_at == j_at), 1.0, 0.0)
    for _ in range(6):
        closure = jnp.minimum(nn_dot(closure.astype(BF16), closure.astype(BF16)), 1.0)
    row = lax.broadcasted_iota(jnp.int32, (128, 64), 0) % 16
    own_node = lax.broadcasted_iota(jnp.int32, (128, 64), 1) == 8 * (row // 2) + 2 * ctx + row % 2
    on_path = nt_dot(jnp.where(own_node, 1.0, 0.0).astype(BF16), closure.astype(BF16))
    tree_bias = (on_path - 1.0) * 1e30

    def by_head(r):
        return (r % 16) * 16 + r // 16

    load_nope.wait()
    load_rope.wait()
    nope_rows = permuted(by_head, nope[...].reshape(256, 128))
    rope_rows = permuted(by_head, rope[...].reshape(256, 64))
    queries[:, 512:576] = rope_rows

    arrived(raw.at[pl.ds(0, 7)], raw_sem.at[0])
    load_slot.wait()
    wanted = slot_ref[dec]
    def key_part(c, t):
        rows = pl.ds(pl.multiple_of((t // 2) * 144, 16), 144)
        return keys.at[rows, pl.ds(pl.multiple_of(c * 256 + (t % 2) * 128, 128), 128)]

    key_part(ctx, tp)[...] = raw[wanted]

    def key_piece(k, t, sem, device):
        c = (ctx + k) % 4
        send(KEYS, key_part(c, t), key_part(c, t), key_sem.at[sem], device)

    def come_key(k, t, sem):
        arrived(key_part((ctx + k) % 4, t), key_sem.at[sem])

    for k in (1, 3, 2):
        key_piece(0, tp, (4 - k) * 4, at_ctx(k))
    def along_y(k):
        if k:
            come_key(k, tp, k * 4)
        for dy in (1, 3, 2):
            key_piece(k, tp, k * 4 + 4 - dy, at_tp(dy))
        key_piece(k, tp, 0, at_tp(0, True))

    def to_other_core(k):
        for dy in (1, 3, 2):
            come_key(k, at_tp(dy)[1], k * 4 + dy)
            key_piece(k, at_tp(dy)[1], 0, at_tp(0, True))

    along_y(0)
    load_key_up.wait()
    for h in range(head_count):
        rows = slice(h * nodes, (h + 1) * nodes)
        queries[rows, 0:512] = nn_dot(nope_rows[rows], key_up[h]).astype(BF16)
    along_y(1)
    along_y(3)
    to_other_core(0)
    along_y(2)
    load_proj.wait()
    proj_t[...] = proj[...].T
    arrived(live.at[pl.ds(0, 7)], raw_sem.at[1])
    position = lax.broadcasted_iota(jnp.int32, (8, 128), 1)
    length = live[wanted]
    bias = jnp.concatenate(
        [jnp.where(position + start < length, 0.0, DEAD)[0:1] for start in range(0, 1024, 128)], axis=1
    )
    for k in (1, 3, 2):
        to_other_core(k)
    arrived(keys.at[pl.ds(0, 288)], key_sem.at[0])

    load_tree.wait()
    load_value_up.wait()

    first_head = [sum(GROUP_HEADS[:g]) for g in range(GROUPS)]

    def attend(g):
        group_heads = GROUP_HEADS[g]
        group_rows = group_heads * nodes
        q = queries[first_head[g] * nodes : first_head[g] * nodes + group_rows, :]
        s = nn_dot(q, keys[...]) * scale + bias
        s_tree = nt_dot(q, tree_rows[...]) * scale + tree_bias[:group_rows]
        peak = jnp.maximum(jnp.max(s, axis=-1, keepdims=True), jnp.max(s_tree, axis=-1, keepdims=True))
        e = jnp.exp(s - peak)
        e_tree = jnp.exp(s_tree - peak)
        total = jnp.sum(e, axis=-1, keepdims=True) + jnp.sum(e_tree, axis=-1, keepdims=True)
        o = nt_dot(e.astype(BF16), keys[0:512, :])
        o = o + nn_dot(e_tree.astype(BF16), tree_rows[:, 0:512])
        o = (o / total).astype(BF16)
        for h in range(group_heads):
            head = first_head[g] + h
            done = nn_dot(o[h * nodes : (h + 1) * nodes], value_up[head]).astype(BF16)
            heads[z * 4 + x, :, head * 128 : (head + 1) * 128] = done


    A, B = 0, 1

    def columns(part, g):
        start = first_head[g] + (0 if part == A else A_HEADS[g])
        count = A_HEADS[g] if part == A else GROUP_HEADS[g] - A_HEADS[g]
        return pl.ds(start * 128, count * 128)

    def block(part, g, dx, dz):
        return heads.at[((z + dz + 8) % 8) * 4 + (x + dx + 4) % 4, :, columns(part, g)]

    def column_blocks(g, dz, first, count):
        return heads.at[pl.ds(((z + dz + 8) % 8) * 4 + first, count), :, columns(A, g)]

    def sem_of(g, name):
        return head_sem.at[g * len(HEAD_SEMS) + HEAD_SEMS.index(name)]

    def go(ref, g, name, dx, dz):
        send(HEADS, ref, ref, sem_of(g, name), at_x(dx, dz))

    def far_side(part, g):
        return 1 if (g % 2 == 0) == (part == B) else -1

    def from_left(g, dz):
        return g % 2 == 0 if dz in (0, -4, 4) else dz < 0

    def distance(dz):
        return "near" if abs(dz) < 2 else "mid" if abs(dz) < 4 else "far"

    def to_x(g, dz):
        ref = block(B, g, 0, dz)
        go(ref, g, f"x{dz}" if from_left(g, dz) else distance(dz), 1, 0)
        go(ref, g, distance(dz) if from_left(g, dz) else f"x{dz}", -1, 0)

    def launch(g):
        own = block(B, g, 0, 0)
        go(own, g, "b-1", 0, 1)
        go(own, g, "b1", 0, -1)
        go(own, g, "b-2", 0, 2)
        go(own, g, "b2", 0, -2)
        for dx in (1, -1, 2):
            go(block(A, g, 0, 0), g, "a", dx, 0)
        to_x(g, 0)

    def a_launch(g):
        arrived(heads.at[pl.ds(0, 3), :, columns(A, g)], sem_of(g, "a"))
        whole = column_blocks(g, 0, 0, 4)
        go(whole, g, "a-1", 0, 1)
        go(whole, g, "a1", 0, -1)

    def b_step(g, dz):
        ref = block(B, g, 0, dz)
        arrived(ref, sem_of(g, f"b{dz}"))
        onward = 1 if dz < 0 else -1
        if abs(dz) == 2:
            go(ref, g, f"b{dz - onward}", 0, onward)
        if abs(dz) == 2 and onward == far_side(B, g):
            go(ref, g, f"b{dz - 2 * onward}", 0, 2 * onward)
        to_x(g, dz)

    def a_step(g, dz):
        onward = 1 if dz < 0 else -1
        half = 0 if onward == 1 else 2
        if abs(dz) == 4:
            arrived(column_blocks(g, dz, half, 2), sem_of(g, f"a{dz}"))
            return
        whole = column_blocks(g, dz, 0, 4)
        arrived(whole, sem_of(g, f"a{dz}"))
        if abs(dz) <= 2:
            go(whole, g, f"a{dz - onward}", 0, onward)
        if abs(dz) == 2:
            go(column_blocks(g, dz, half, 2), g, f"a{dz - 2 * onward}", 0, 2 * onward)

    def x_step(g, dz):
        dx = -1 if from_left(g, dz) else 1
        ref = block(B, g, dx, dz)
        arrived(ref, sem_of(g, f"x{dz}"))
        go(ref, g, distance(dz), -dx, 0)

    def project(k):
        origin = (ctx + k) % 4
        rows = heads[pl.ds(origin * 8, 8)].reshape(128, 2048)
        product = nn_dot(rows, proj_t[...]).astype(BF16)
        partial[origin] = permuted(by_target, product).reshape(8, 16, 224)
        sums[origin, tp] = partial[origin, tp]
        for dy in (2, 1, 3, 0):
            for other in (False, True):
                if dy or other:
                    device = at_tp(dy, other)
                    send(SUMS, partial.at[origin, device[1]], sums.at[origin, tp], raw_sem.at[3 if k == 2 else 2], device)

    def by_target(r):
        j, rest = r // 16, r % 16
        return (rest // 2) * 16 + 2 * j + rest % 2

    def opposite(name, count):
        for g in range(GROUPS):
            arrived(heads.at[pl.ds(0, count), :, columns(B, g)], sem_of(g, name))

    for what, *which in ORDER:
        if what == "L":
            attend(*which)
            launch(*which)
        elif what == "P":
            if which[0] == 0:
                opposite("near", 6)
                project(0)
            else:
                opposite("mid", 8)
                project(1)
                project(3)
        else:
            {"a": a_launch, "A": a_step, "b": b_step, "x": x_step}[what](*which)
    opposite("far", 2)
    project(2)
    every = sums.reshape(32, 16, 224)
    arrived(every.at[pl.ds(0, 21)], raw_sem.at[2])
    for k in (0, 1, 3, 2):
        if k == 2:
            arrived(every.at[pl.ds(0, 7)], raw_sem.at[3])
        origin = (ctx + k) % 4
        total = jnp.zeros((16, 224), F32)
        for source in range(8):
            total = total + sums[origin, source].astype(F32)
        totals[origin] = total.astype(BF16)

    def by_slot(r):
        return ((r // 2) % 4) * 16 + ((r // 8) % 2) * 8 + (r // 16) * 2 + r % 2

    out_ref[...] = permuted(by_slot, totals[...].reshape(64, 224))
    all_sent(LIVE, live.at[pl.ds(0, 7)])
    all_sent(RAW, raw.at[pl.ds(0, 7)])
    all_sent(KEYS, value_up.reshape(8192, 128).at[pl.ds(0, 31 * 144)])
    all_sent(HEADS, heads.at[pl.ds(0, 31)])
    all_sent(SUMS, every.at[pl.ds(0, 28)])


def on_device(cache, lengths, slots, parents, nope, rope, latent_rows, key_up, value_up, proj):
    anywhere = pl.BlockSpec(memory_space=pl.ANY)
    in_vmem = pl.BlockSpec(memory_space=pltpu.VMEM)
    dma = pltpu.SemaphoreType.DMA
    out = pl.pallas_call(
        kernel,
        out_shape=jax.ShapeDtypeStruct((64, 224), BF16),
        in_specs=[anywhere, pl.BlockSpec(memory_space=pltpu.SMEM)] + [anywhere] * 8,
        out_specs=in_vmem,
        scratch_shapes=[
            pltpu.SMEM((8,), jnp.int32),
            pltpu.VMEM((8, 144, 128), BF16),
            pltpu.VMEM((8, 8, 128), jnp.int32),
            pltpu.VMEM((576, 1024), BF16),
            pltpu.VMEM((1, 64), jnp.int32),
            pltpu.VMEM((8, 2, 16, 128), BF16),
            pltpu.VMEM((8, 2, 16, 64), BF16),
            pltpu.VMEM((64, 576), BF16),
            pltpu.VMEM((16, 128, 512), BF16),
            pltpu.VMEM((16, 512, 128), BF16),
            pltpu.VMEM((224, 2048), BF16),
            pltpu.VMEM((2048, 224), BF16),
            pltpu.VMEM((256, 576), BF16),
            pltpu.VMEM((32, 16, 2048), BF16),
            pltpu.VMEM((4, 8, 16, 224), BF16),
            pltpu.VMEM((4, 8, 16, 224), BF16),
            pltpu.VMEM((4, 16, 224), BF16),
            dma((9,)), dma((4,)), dma((16,)), dma((GROUPS * len(HEAD_SEMS),)), dma((5,)),
        ],
        compiler_params=pltpu.CompilerParams(
            collective_id=0, has_side_effects=True, vmem_limit_bytes=58 * 1024 * 1024
        ),
        name="tree_attention",
    )(
        cache[0].T, lengths, slots, parents,
        nope.reshape(8, 8, 16, 128), rope.reshape(8, 8, 16, 64), latent_rows.reshape(latent_rows.shape[1:]),
        key_up, value_up, proj.T,
    )
    return out.reshape(8, 8, 224)


def solution(mesh):
    return jax.shard_map(
        on_device,
        mesh=mesh,
        in_specs=(
            P("dec", "ctx", None),
            P("dec"),
            P(),
            P("dec", None),
            P("dec", None, "tp", None),
            P("dec", None, "tp", None),
            P("dec", None, None),
            P("tp", None, None),
            P("tp", None, None),
            P("tp", ("ctx", "dec")),
        ),
        out_specs=P(None, "tp", ("ctx", "dec")),
        check_vma=False,
    )
```

```python
import math

import jax
import jax.numpy as jnp
from jax import lax
from jax.experimental import pallas as pl
from jax.experimental.pallas import tpu as pltpu
from jax.sharding import PartitionSpec as P

MESH = pl.DeviceIdType.MESH
F32 = jnp.float32
BF16 = jnp.bfloat16
GROUP_HEADS = (8, 8)
A_HEADS = (3, 3)
GROUPS = len(GROUP_HEADS)
DEAD = -1e30
OFFSETS = [0, -1, 1, -2, 2, -3, 3, -4, 4]
HEAD_SEMS = ["a", "near", "mid", "far"]
HEAD_SEMS += [f"{part}{dz}" for part in ("a", "b") for dz in OFFSETS[1:]]
HEAD_SEMS += [f"x{dz}" for dz in OFFSETS]

ORDER = [
    ("L", 0), ("L", 1), ("b", 0, -1), ("b", 0, 1), ("a", 0), ("x", 0, 0), ("b", 0, -2), ("b", 0, 2), ("b", 1, -1),
    ("b", 1, 1), ("a", 1), ("x", 1, 0), ("x", 0, -1), ("b", 1, -2), ("b", 1, 2), ("x", 0, 1), ("A", 0, -1),
    ("A", 0, 1), ("x", 0, -2), ("b", 0, -3), ("b", 0, 3), ("x", 0, 2), ("x", 1, -1), ("x", 1, 1), ("b", 0, -4),
    ("A", 1, 1), ("b", 1, 3), ("A", 1, -1), ("x", 1, -2), ("x", 1, 2), ("b", 1, -3), ("b", 1, 4), ("A", 0, -2),
    ("x", 0, -3), ("A", 0, 2), ("x", 0, 3), ("A", 1, 2), ("x", 0, -4), ("A", 1, -2), ("x", 1, 3), ("x", 1, -3),
    ("P", 0), ("A", 0, -3), ("x", 1, 4), ("A", 0, 3), ("A", 0, -4), ("A", 0, 4), ("A", 1, -3), ("A", 1, 3), ("P", 1),
    ("A", 1, -4), ("A", 1, 4),
]


def nt_dot(a, b):
    return lax.dot_general(a, b, (((1,), (1,)), ((), ())), preferred_element_type=F32)


def nn_dot(a, b):
    return jnp.dot(a, b, preferred_element_type=F32)


def permuted(source_of, value):
    rows = value.shape[0]
    r = lax.broadcasted_iota(jnp.int32, (rows, rows), 0)
    s = lax.broadcasted_iota(jnp.int32, (rows, rows), 1)
    select = jnp.where(source_of(r) == s, 1.0, 0.0).astype(BF16)
    return nn_dot(select, value).astype(BF16)


def kernel(
    cache_ref, length_ref, slots_ref, parents_ref, nope_ref, rope_ref, latent_ref, key_up_ref, value_up_ref, proj_ref,
    out_ref,
    slot_ref, raw, live, keys, parents, nope, rope, tree_rows, key_up, value_up, proj, proj_t, queries, heads, partial, sums, totals,
    local_sem, raw_sem, key_sem, head_sem, send_sem,
):
    ctx, tp, dec = lax.axis_index("ctx"), lax.axis_index("tp"), lax.axis_index("dec")
    x, z_lo = dec // 2, dec % 2
    y, core = tp // 2, tp % 2
    z = ctx * 2 + z_lo
    nodes, head_count = 16, 16
    scale = 1.0 / math.sqrt(192.0)

    def at_x(dx, dz=0):
        xx, zz = (x + dx + 4) % 4, (z + dz + 8) % 8
        return (zz // 2, tp, xx * 2 + zz % 2)

    def at_tp(dy, other_core=False):
        core_there = 1 - core if other_core else core
        return (ctx, ((y + dy) % 4) * 2 + core_there, dec)

    def at_dec(k):
        return (ctx, tp, (dec + k) % 8)

    def at_ctx(k):
        return ((ctx + k) % 4, tp, dec)

    peers = [at_dec(k) for k in range(1, 8)]
    peers += [at_ctx(k) for k in range(1, 4)]
    peers += [at_tp(dy) for dy in (1, 2, 3)] + [at_tp(0, True)]

    LIVE, RAW, KEYS, HEADS, SUMS = range(5)

    def described(src, dst, kind, sem, device):
        return pltpu.make_async_remote_copy(
            src_ref=src, dst_ref=dst, send_sem=send_sem.at[kind], recv_sem=sem,
            device_id=device, device_id_type=MESH,
        )

    def send(kind, ref, dst, sem, device):
        described(ref, dst, kind, sem, device).start()

    def arrived(dst, sem):
        described(dst, dst, 0, sem, at_dec(1)).wait_recv()

    def all_sent(kind, as_many_bytes):
        described(as_many_bytes, as_many_bytes, kind, raw_sem.at[0], at_dec(1)).wait_send()

    loads = []

    def load(src, dst):
        copy = pltpu.make_async_copy(src, dst, local_sem.at[len(loads)])
        copy.start()
        loads.append(copy)
        return copy

    own_rows = cache_ref.at[pl.ds(pl.multiple_of(y * 144, 16), 144), pl.ds(pl.multiple_of(core * 128, 128), 128)]
    load_slot = load(slots_ref, slot_ref)
    load_raw = load(own_rows, raw.at[dec])
    load_nope = load(nope_ref.at[:, pl.ds(ctx * 2, 2)], nope)
    load_rope = load(rope_ref.at[:, pl.ds(ctx * 2, 2)], rope)
    load_parents = load(parents_ref, parents)
    load_tree = load(latent_ref, tree_rows)
    load_key_up = load(key_up_ref, key_up)
    load_value_up = load(value_up_ref, value_up)
    load_proj = load(proj_ref, proj)

    barrier = pltpu.get_barrier_semaphore()
    for peer in peers:
        pl.semaphore_signal(barrier, inc=1, device_id=peer, device_id_type=MESH)
    live[dec] = jnp.full((8, 128), length_ref[0], jnp.int32)
    pl.semaphore_wait(barrier, len(peers))

    load_raw.wait()
    for k in range(1, 8):
        send(RAW, raw.at[dec], raw.at[dec], raw_sem.at[0], at_dec(k))
    for k in range(1, 8):
        send(LIVE, live.at[dec], live.at[dec], raw_sem.at[1], at_dec(k))

    j_at = lax.broadcasted_iota(jnp.int32, (64, 64), 0)
    i_at = lax.broadcasted_iota(jnp.int32, (64, 64), 1)
    load_parents.wait()
    closure = jnp.where((parents[...] == j_at) | (i_at == j_at), 1.0, 0.0)
    for _ in range(6):
        closure = jnp.minimum(nn_dot(closure.astype(BF16), closure.astype(BF16)), 1.0)
    row = lax.broadcasted_iota(jnp.int32, (128, 64), 0) % 16
    own_node = lax.broadcasted_iota(jnp.int32, (128, 64), 1) == 8 * (row // 2) + 2 * ctx + row % 2
    on_path = nt_dot(jnp.where(own_node, 1.0, 0.0).astype(BF16), closure.astype(BF16))
    tree_bias = (on_path - 1.0) * 1e30

    def by_head(r):
        return (r % 16) * 16 + r // 16

    load_nope.wait()
    load_rope.wait()
    nope_rows = permuted(by_head, nope[...].reshape(256, 128))
    rope_rows = permuted(by_head, rope[...].reshape(256, 64))
    queries[:, 512:576] = rope_rows

    arrived(raw.at[pl.ds(0, 7)], raw_sem.at[0])
    load_slot.wait()
    wanted = slot_ref[dec]
    def key_part(c, t):
        rows = pl.ds(pl.multiple_of((t // 2) * 144, 16), 144)
        return keys.at[rows, pl.ds(pl.multiple_of(c * 256 + (t % 2) * 128, 128), 128)]

    key_part(ctx, tp)[...] = raw[wanted]

    def key_piece(k, t, sem, device):
        c = (ctx + k) % 4
        send(KEYS, key_part(c, t), key_part(c, t), key_sem.at[sem], device)

    def come_key(k, t, sem):
        arrived(key_part((ctx + k) % 4, t), key_sem.at[sem])

    for k in (1, 3, 2):
        key_piece(0, tp, (4 - k) * 4, at_ctx(k))
    def along_y(k):
        if k:
            come_key(k, tp, k * 4)
        for dy in (1, 3, 2):
            key_piece(k, tp, k * 4 + 4 - dy, at_tp(dy))
        key_piece(k, tp, 0, at_tp(0, True))

    def to_other_core(k):
        for dy in (1, 3, 2):
            come_key(k, at_tp(dy)[1], k * 4 + dy)
            key_piece(k, at_tp(dy)[1], 0, at_tp(0, True))

    along_y(0)
    load_key_up.wait()
    for h in range(head_count):
        rows = slice(h * nodes, (h + 1) * nodes)
        queries[rows, 0:512] = nn_dot(nope_rows[rows], key_up[h]).astype(BF16)
    along_y(1)
    along_y(3)
    to_other_core(0)
    along_y(2)
    load_proj.wait()
    proj_t[...] = proj[...].T
    arrived(live.at[pl.ds(0, 7)], raw_sem.at[1])
    position = lax.broadcasted_iota(jnp.int32, (8, 128), 1)
    length = live[wanted]
    bias = jnp.concatenate(
        [jnp.where(position + start < length, 0.0, DEAD)[0:1] for start in range(0, 1024, 128)], axis=1
    )
    for k in (1, 3, 2):
        to_other_core(k)
    arrived(keys.at[pl.ds(0, 288)], key_sem.at[0])

    load_tree.wait()
    load_value_up.wait()

    first_head = [sum(GROUP_HEADS[:g]) for g in range(GROUPS)]

    def attend(g):
        group_heads = GROUP_HEADS[g]
        group_rows = group_heads * nodes
        q = queries[first_head[g] * nodes : first_head[g] * nodes + group_rows, :]
        s = nn_dot(q, keys[...]) * scale + bias
        s_tree = nt_dot(q, tree_rows[...]) * scale + tree_bias[:group_rows]
        peak = jnp.maximum(jnp.max(s, axis=-1, keepdims=True), jnp.max(s_tree, axis=-1, keepdims=True))
        e = jnp.exp(s - peak)
        e_tree = jnp.exp(s_tree - peak)
        total = jnp.sum(e, axis=-1, keepdims=True) + jnp.sum(e_tree, axis=-1, keepdims=True)
        o = nt_dot(e.astype(BF16), keys[0:512, :])
        o = o + nn_dot(e_tree.astype(BF16), tree_rows[:, 0:512])
        o = (o * (1.0 / total)).astype(BF16)
        for h in range(group_heads):
            head = first_head[g] + h
            done = nn_dot(o[h * nodes : (h + 1) * nodes], value_up[head]).astype(BF16)
            heads[z * 4 + x, :, head * 128 : (head + 1) * 128] = done


    A, B = 0, 1

    def columns(part, g):
        start = first_head[g] + (0 if part == A else A_HEADS[g])
        count = A_HEADS[g] if part == A else GROUP_HEADS[g] - A_HEADS[g]
        return pl.ds(start * 128, count * 128)

    def block(part, g, dx, dz):
        return heads.at[((z + dz + 8) % 8) * 4 + (x + dx + 4) % 4, :, columns(part, g)]

    def column_blocks(g, dz, first, count):
        return heads.at[pl.ds(((z + dz + 8) % 8) * 4 + first, count), :, columns(A, g)]

    def sem_of(g, name):
        return head_sem.at[g * len(HEAD_SEMS) + HEAD_SEMS.index(name)]

    def go(ref, g, name, dx, dz):
        send(HEADS, ref, ref, sem_of(g, name), at_x(dx, dz))

    def far_side(part, g):
        return 1 if (g % 2 == 0) == (part == B) else -1

    def from_left(g, dz):
        return g % 2 == 0 if dz in (0, -4, 4) else dz < 0

    def distance(dz):
        return "near" if abs(dz) < 2 else "mid" if abs(dz) < 4 else "far"

    def to_x(g, dz):
        ref = block(B, g, 0, dz)
        go(ref, g, f"x{dz}" if from_left(g, dz) else distance(dz), 1, 0)
        go(ref, g, distance(dz) if from_left(g, dz) else f"x{dz}", -1, 0)

    def launch(g):
        own = block(B, g, 0, 0)
        go(own, g, "b-1", 0, 1)
        go(own, g, "b1", 0, -1)
        go(own, g, "b-2", 0, 2)
        go(own, g, "b2", 0, -2)
        for dx in (1, -1, 2):
            go(block(A, g, 0, 0), g, "a", dx, 0)
        to_x(g, 0)

    def a_launch(g):
        arrived(heads.at[pl.ds(0, 3), :, columns(A, g)], sem_of(g, "a"))
        whole = column_blocks(g, 0, 0, 4)
        go(whole, g, "a-1", 0, 1)
        go(whole, g, "a1", 0, -1)

    def b_step(g, dz):
        ref = block(B, g, 0, dz)
        arrived(ref, sem_of(g, f"b{dz}"))
        onward = 1 if dz < 0 else -1
        if abs(dz) == 2:
            go(ref, g, f"b{dz - onward}", 0, onward)
        if abs(dz) == 2 and onward == far_side(B, g):
            go(ref, g, f"b{dz - 2 * onward}", 0, 2 * onward)
        to_x(g, dz)

    def a_step(g, dz):
        onward = 1 if dz < 0 else -1
        half = 0 if onward == 1 else 2
        if abs(dz) == 4:
            arrived(column_blocks(g, dz, half, 2), sem_of(g, f"a{dz}"))
            return
        whole = column_blocks(g, dz, 0, 4)
        arrived(whole, sem_of(g, f"a{dz}"))
        if abs(dz) <= 2:
            go(whole, g, f"a{dz - onward}", 0, onward)
        if abs(dz) == 2:
            go(column_blocks(g, dz, half, 2), g, f"a{dz - 2 * onward}", 0, 2 * onward)

    def x_step(g, dz):
        dx = -1 if from_left(g, dz) else 1
        ref = block(B, g, dx, dz)
        arrived(ref, sem_of(g, f"x{dz}"))
        go(ref, g, distance(dz), -dx, 0)

    def project(k):
        origin = (ctx + k) % 4
        rows = heads[pl.ds(origin * 8, 8)].reshape(128, 2048)
        product = nn_dot(rows, proj_t[...]).astype(BF16)
        partial[origin] = permuted(by_target, product).reshape(8, 16, 224)
        sums[origin, tp] = partial[origin, tp]
        for dy in (2, 1, 3, 0):
            for other in (False, True):
                if dy or other:
                    device = at_tp(dy, other)
                    send(SUMS, partial.at[origin, device[1]], sums.at[origin, tp], raw_sem.at[3 if k == 2 else 2], device)

    def by_target(r):
        j, rest = r // 16, r % 16
        return (rest // 2) * 16 + 2 * j + rest % 2

    def opposite(name, count):
        for g in range(GROUPS):
            arrived(heads.at[pl.ds(0, count), :, columns(B, g)], sem_of(g, name))

    for what, *which in ORDER:
        if what == "L":
            attend(*which)
            launch(*which)
        elif what == "P":
            if which[0] == 0:
                opposite("near", 6)
                project(0)
            else:
                opposite("mid", 8)
                project(1)
                project(3)
        else:
            {"a": a_launch, "A": a_step, "b": b_step, "x": x_step}[what](*which)
    opposite("far", 2)
    project(2)
    every = sums.reshape(32, 16, 224)
    arrived(every.at[pl.ds(0, 21)], raw_sem.at[2])
    for k in (0, 1, 3, 2):
        if k == 2:
            arrived(every.at[pl.ds(0, 7)], raw_sem.at[3])
        origin = (ctx + k) % 4
        total = jnp.zeros((16, 224), F32)
        for source in range(8):
            total = total + sums[origin, source].astype(F32)
        totals[origin] = total.astype(BF16)

    def by_slot(r):
        return ((r // 2) % 4) * 16 + ((r // 8) % 2) * 8 + (r // 16) * 2 + r % 2

    out_ref[...] = permuted(by_slot, totals[...].reshape(64, 224))
    all_sent(LIVE, live.at[pl.ds(0, 7)])
    all_sent(RAW, raw.at[pl.ds(0, 7)])
    all_sent(KEYS, value_up.reshape(8192, 128).at[pl.ds(0, 31 * 144)])
    all_sent(HEADS, heads.at[pl.ds(0, 31)])
    all_sent(SUMS, every.at[pl.ds(0, 28)])


def on_device(cache, lengths, slots, parents, nope, rope, latent_rows, key_up, value_up, proj):
    anywhere = pl.BlockSpec(memory_space=pl.ANY)
    in_vmem = pl.BlockSpec(memory_space=pltpu.VMEM)
    dma = pltpu.SemaphoreType.DMA
    out = pl.pallas_call(
        kernel,
        out_shape=jax.ShapeDtypeStruct((64, 224), BF16),
        in_specs=[anywhere, pl.BlockSpec(memory_space=pltpu.SMEM)] + [anywhere] * 8,
        out_specs=in_vmem,
        scratch_shapes=[
            pltpu.SMEM((8,), jnp.int32),
            pltpu.VMEM((8, 144, 128), BF16),
            pltpu.VMEM((8, 8, 128), jnp.int32),
            pltpu.VMEM((576, 1024), BF16),
            pltpu.VMEM((1, 64), jnp.int32),
            pltpu.VMEM((8, 2, 16, 128), BF16),
            pltpu.VMEM((8, 2, 16, 64), BF16),
            pltpu.VMEM((64, 576), BF16),
            pltpu.VMEM((16, 128, 512), BF16),
            pltpu.VMEM((16, 512, 128), BF16),
            pltpu.VMEM((224, 2048), BF16),
            pltpu.VMEM((2048, 224), BF16),
            pltpu.VMEM((256, 576), BF16),
            pltpu.VMEM((32, 16, 2048), BF16),
            pltpu.VMEM((4, 8, 16, 224), BF16),
            pltpu.VMEM((4, 8, 16, 224), BF16),
            pltpu.VMEM((4, 16, 224), BF16),
            dma((9,)), dma((4,)), dma((16,)), dma((GROUPS * len(HEAD_SEMS),)), dma((5,)),
        ],
        compiler_params=pltpu.CompilerParams(
            collective_id=0, has_side_effects=True, vmem_limit_bytes=58 * 1024 * 1024
        ),
        name="tree_attention",
    )(
        cache[0].T, lengths, slots, parents,
        nope.reshape(8, 8, 16, 128), rope.reshape(8, 8, 16, 64), latent_rows.reshape(latent_rows.shape[1:]),
        key_up, value_up, proj.T,
    )
    return out.reshape(8, 8, 224)


def solution(mesh):
    return jax.shard_map(
        on_device,
        mesh=mesh,
        in_specs=(
            P("dec", "ctx", None),
            P("dec"),
            P(),
            P("dec", None),
            P("dec", None, "tp", None),
            P("dec", None, "tp", None),
            P("dec", None, None),
            P("tp", None, None),
            P("tp", None, None),
            P("tp", ("ctx", "dec")),
        ),
        out_specs=P(None, "tp", ("ctx", "dec")),
        check_vma=False,
    )
```
